32 devices in a mesh: lat: 8 (over z, y), lon: 4 (over x, core).
Axes of the slice: x: 2, y: 2, z: 4, core: 2. Of those that a mesh axis runs over, the one named last changes fastest.
Arguments:
- field: bfloat16 [64, 1440, 256], P('lat', 'lon'), may hold values from -6 to 6
- cotangent: bfloat16 [64, 1440, 256], P('lat', 'lon'), may hold values from -0.118585412 to 0.118585412
- legendre: bfloat16 [384, 64, 384], P('lat'), may hold values from -0.75 to 0.75
- quad_weight: float32 [64], P('lat'), may hold values from 0.25 to 2
- order_slots: int32 [384], replicated, may hold values from 0 to 383, as said below
- support_blocks: int32 [8, 3], P('lat'), may hold values from 0 to 7, as said below
- filter_values: bfloat16 [3, 64, 3, 8], P(None, 'lat'), may hold values from -1.25 to 1.25
- spectral_weight: bfloat16 [2, 256, 256], replicated, may hold values from -0.25 to 0.25
- disco_weight: bfloat16 [3, 256, 256], replicated, may hold values from -0.21875 to 0.21875
Outputs:
- output: bfloat16 [64, 1440, 256], P('lat', 'lon')
- grad_spectral: float32 [2, 256, 256], replicated
- grad_disco: float32 [3, 256, 256], replicated
The draws below stay inside these ranges and needn't reach their ends.
Inputs may be any that keep to these rules, and one draw needn't show every extreme that they name: order_slots holds every order from 0 to 383 exactly once; the first slot of each block of 384 // 8 slots holds an order below 8. `support_blocks`: slot 0 of row block b names b itself; slots 1 and 2 name b - 1, b or b + 1.
All inputs are finite; a program needn't handle non-finite values.
Results may differ from the reference program's by a relative error of at most 0.015.
Values may be sent and summed in bfloat16 or wider, within the bound.
A program may use at most 128 MiB of HBM per device.

```python
import math
import jax
import jax.numpy as jnp
from jax import lax

C = 256
NLON = 1440
MMAX = 384
LMAX = 384
LAT_DEV = 8
NLAT = 64
LBLOCKS = 8


def draw_order_slots(key, part):
    key = jax.random.fold_in(key, 23)
    low_key = jax.random.fold_in(key, 1)
    rest_key = jax.random.fold_in(key, 2)
    per_block = MMAX // LBLOCKS
    low_orders = jax.random.permutation(low_key, jnp.arange(LBLOCKS, dtype=jnp.int32))
    rest_orders = jax.random.permutation(rest_key, jnp.arange(LBLOCKS, MMAX, dtype=jnp.int32))
    rest_orders = rest_orders.reshape(LBLOCKS, per_block - 1)
    table = jnp.concatenate([low_orders[:, None], rest_orders], axis=1)
    return table.reshape(MMAX).astype(jnp.int32)


def draw_support_blocks(key, part):
    key = jax.random.fold_in(key, 11)
    rows = jnp.arange(LBLOCKS, dtype=jnp.int32)
    offsets = jax.random.randint(key, (LBLOCKS, 2), -1, 2, dtype=jnp.int32)
    others = jnp.clip(rows[:, None] + offsets, 0, LBLOCKS - 1)
    return jnp.concatenate([rows[:, None], others], axis=1).astype(jnp.int32)


def draw_cotangent(key, part):
    key = jax.random.fold_in(key, 37)
    values = jnp.clip(jax.random.normal(key, (NLAT, NLON, C), jnp.float32), -6.0, 6.0)
    band = (jnp.arange(NLAT, dtype=jnp.int32) // LAT_DEV).astype(jnp.float32)
    rows = jnp.exp(band / (LBLOCKS - 1.0) * jnp.log(3.0))
    scale = 1.0 / jnp.sqrt(2.0 * LAT_DEV * NLON)
    return (values * rows[:, None, None] * scale).astype(jnp.bfloat16)


def level_of(stream_key, extent, cuts, low, largest):
    loudness, own = 1.0, jax.random.fold_in(stream_key, 6)
    for dim, parts in cuts:
        heights = jnp.exp(jax.random.uniform(jax.random.fold_in(own, dim), (parts,), jnp.float32, low / len(cuts), largest / len(cuts)))
        loudness = loudness * jnp.repeat(heights, extent[dim] // parts).reshape([-1 if axis == dim else 1 for axis in range(len(extent))])
    return loudness


def noise(rng, extent, width, reach, pieces=(), kind=jnp.bfloat16):
    values = width * jax.random.normal(rng, extent, jnp.float32)
    if pieces:
        values = values * level_of(rng, extent, pieces, -0.22, 0.18)
    return jnp.clip(values, -reach, reach).astype(kind)


def setup_inputs(seed: int = 0) -> dict:
    splits = jax.random.split(jax.random.key(seed), 10)
    return {
        "field": noise(splits[0], (NLAT, NLON, C), 1.0, 6.0, ((0, 8), (1, 4))),
        "cotangent": draw_cotangent(jax.random.fold_in(splits[9], 71), 0),
        "legendre": noise(splits[2], (MMAX, NLAT, LMAX), NLAT ** -0.5, 0.75, ((0, 8),)),
        "quad_weight": jnp.clip(jnp.exp(math.log(2.0) - 2.0794415 * jax.random.uniform(splits[3], (NLAT,), jnp.float32) ** level_of(splits[3], (NLAT,), ((0, 8),), -0.2, 0.2)), 0.25, 2.0),
        "order_slots": draw_order_slots(jax.random.fold_in(splits[9], 71), 0),
        "support_blocks": draw_support_blocks(jax.random.fold_in(splits[9], 71), 0),
        "filter_values": noise(splits[6], (3, NLAT, 3, LAT_DEV), (3 * LAT_DEV) ** -0.5, 1.25, ((1, 8),)),
        "spectral_weight": noise(splits[7], (2, C, C), (2 * C) ** -0.5, 0.25),
        "disco_weight": noise(splits[8], (3, C, C), (3 * C) ** -0.5, 0.21875),
    }


def fourier_tables(order_slots, nlon):
    column = jnp.arange(nlon, dtype=jnp.int32)
    phase = column[:, None] * order_slots.astype(jnp.int32)[None, :] % nlon
    angle = phase.astype(jnp.float32) * (2.0 * jnp.pi / nlon)
    cosine = jnp.cos(angle)
    sine = jnp.sin(angle)
    factor = jnp.where(order_slots == 0, 1.0, 2.0).astype(jnp.float32)[None, :]
    analysis_table = jnp.concatenate([cosine / nlon, -sine / nlon], axis=1).astype(jnp.bfloat16)
    synthesis_table = jnp.concatenate([factor * cosine, -factor * sine], axis=1).astype(jnp.bfloat16)
    return (analysis_table, synthesis_table)

def reference(field, cotangent, legendre, quad_weight, order_slots, support_blocks, filter_values, spectral_weight, disco_weight):
    f32 = jnp.float32
    bf16 = jnp.bfloat16
    analysis_table, synthesis_table = fourier_tables(order_slots, NLON)
    degree_mask = (jnp.arange(LMAX, dtype=jnp.int32)[None, :] >= order_slots[:, None]).astype(f32)
    legendre_full = legendre.astype(f32)

    def longitude(values, table):
        flat = values.transpose(0, 2, 1).reshape(NLAT * C, NLON)
        return jnp.dot(flat, table, preferred_element_type=f32).reshape(NLAT, C, 2, MMAX)

    def project(spec):
        coeffs = jnp.einsum('kal,acrk->klrc', legendre_full, spec.astype(f32))
        return (coeffs * degree_mask[:, :, None, None]).astype(bf16)
    spectrum = (longitude(field, analysis_table) * quad_weight[:, None, None, None]).astype(bf16)
    coeffs = project(spectrum)
    real_part = coeffs[:, :, 0].reshape(-1, C)
    imag_part = coeffs[:, :, 1].reshape(-1, C)
    w_real = spectral_weight[0]
    w_imag = spectral_weight[1]
    out_real = jnp.dot(real_part, w_real, preferred_element_type=f32) - jnp.dot(imag_part, w_imag, preferred_element_type=f32)
    out_imag = jnp.dot(real_part, w_imag, preferred_element_type=f32) + jnp.dot(imag_part, w_real, preferred_element_type=f32)
    mixed = jnp.stack([out_real.reshape(MMAX, LMAX, C), out_imag.reshape(MMAX, LMAX, C)], axis=2).astype(bf16)
    masked = mixed.astype(f32) * degree_mask[:, :, None, None]
    grid_spectrum = jnp.einsum('kal,klrc->arkc', legendre_full, masked).astype(bf16)
    flat_grid = grid_spectrum.reshape(NLAT, 2 * MMAX, C).transpose(0, 2, 1).reshape(NLAT * C, 2 * MMAX)
    spectral_out = jnp.dot(flat_grid, synthesis_table.T, preferred_element_type=f32)
    spectral_out = spectral_out.reshape(NLAT, C, NLON).transpose(0, 2, 1).astype(bf16)
    padded = jnp.concatenate([field[:, -1:], field, field[:, :1]], axis=1)
    padded = jnp.pad(padded, ((LAT_DEV, LAT_DEV), (0, 0), (0, 0)))
    block_ids = jnp.arange(LBLOCKS, dtype=jnp.int32)
    picks = support_blocks - block_ids[:, None] + 1
    onehot = (picks[:, :, None] == jnp.arange(3, dtype=jnp.int32)[None, None, :]).astype(f32)
    psi = filter_values.astype(f32).reshape(3, LBLOCKS, LAT_DEV, 3, LAT_DEV)
    operators = jnp.einsum('tnasb,nsq->ntaqb', psi, onehot).reshape(LBLOCKS, 3, LAT_DEV, 3 * LAT_DEV).astype(bf16)

    def responses(block):
        window_rows = lax.dynamic_slice_in_dim(padded, (block * LAT_DEV).astype(jnp.int32), 3 * LAT_DEV, 0)
        block_ops = operators[block]
        result = []
        for tap in range(3):
            piece = jnp.einsum('ab,boc->aoc', block_ops[tap].astype(f32), window_rows[:, tap:tap + NLON].astype(f32))
            result.append(piece.astype(bf16))
        return result

    def disco_block(block):
        resp = responses(block)
        total = jnp.zeros((LAT_DEV * NLON, C), f32)
        for tap in range(3):
            total = total + jnp.dot(resp[tap].reshape(-1, C), disco_weight[tap], preferred_element_type=f32)
        return total.reshape(LAT_DEV, NLON, C)
    disco_sum = lax.map(disco_block, block_ids).reshape(NLAT, NLON, C)
    pre_act = spectral_out.astype(f32) + disco_sum
    activated, pullback = jax.vjp(jax.nn.gelu, pre_act)
    output = (field.astype(f32) + activated).astype(bf16)
    grad_pre, = pullback(cotangent.astype(f32))
    grad_pre = grad_pre.astype(bf16)

    def accumulate(carry, block):
        resp = responses(block)
        rows = lax.dynamic_slice_in_dim(grad_pre, (block * LAT_DEV).astype(jnp.int32), LAT_DEV, 0).reshape(-1, C)
        terms = jnp.stack([jnp.dot(resp[tap].reshape(-1, C).T, rows, preferred_element_type=f32) for tap in range(3)])
        return (carry + terms, None)
    grad_disco, _ = lax.scan(accumulate, jnp.zeros((3, C, C), f32), block_ids)
    grad_grid = longitude(grad_pre, synthesis_table).astype(bf16)
    grad_coeffs = project(grad_grid)
    grad_real = grad_coeffs[:, :, 0].reshape(-1, C)
    grad_imag = grad_coeffs[:, :, 1].reshape(-1, C)
    g_real = jnp.dot(real_part.T, grad_real, preferred_element_type=f32) + jnp.dot(imag_part.T, grad_imag, preferred_element_type=f32)
    g_imag = jnp.dot(real_part.T, grad_imag, preferred_element_type=f32) - jnp.dot(imag_part.T, grad_real, preferred_element_type=f32)
    grad_spectral = jnp.stack([g_real, g_imag])
    return (output, grad_spectral, grad_disco)
```

```python
import jax
import jax.numpy as jnp
from jax import lax
from jax.sharding import PartitionSpec as P

BOTH = ("lat", "lon")


def padded(value, sides, width, wrap):
    for axis, dim in sides:
        size, length = (lax.axis_size(axis), value.shape[dim])
        up = [(i, (i + 1) % size) for i in range(size if wrap else size - 1)]
        down = [(j, i) for i, j in up]
        last = lax.slice_in_dim(value, length - width, length, axis=dim)
        leading = lax.slice_in_dim(value, 0, width, axis=dim)
        before = lax.ppermute(last, axis, up)
        after = lax.ppermute(leading, axis, down)
        value = jnp.concatenate([before, value, after], axis=dim)
    return value


def outer_sum(left, right):
    return lax.dot_general(
        left, right, (((0,), (0,)), ((), ())), preferred_element_type=jnp.float32
    )


def local(
    field,
    cotangent,
    legendre,
    quad_weight,
    order_slots,
    support_blocks,
    filter_values,
    spectral_weight,
    disco_weight,
):
    f32 = jnp.float32
    bf16 = jnp.bfloat16
    lat_rows, lon_cols, channels = field.shape
    n_lon = lax.axis_size("lon")
    n_dev = n_lon * lax.axis_size("lat")
    nlon = lon_cols * n_lon
    slots_dev, nlat, degrees = legendre.shape
    own_rows = lat_rows // n_lon
    lat_pos = lax.axis_index("lat")
    lon_pos = lax.axis_index("lon")
    own = -(-slots_dev // n_lon)
    pad = own * n_lon - slots_dev

    orders = order_slots.reshape(-1, slots_dev)
    orders = jnp.pad(orders, ((0, 0), (0, pad))).reshape(n_dev, own)
    flat_orders = orders.reshape(-1)
    column = jnp.arange(nlon, dtype=jnp.int32)
    phase = column[:, None] * flat_orders[None, :] % nlon
    angle = phase.astype(f32) * (2.0 * jnp.pi / nlon)
    cosine = jnp.cos(angle).astype(bf16).reshape(nlon, n_dev, own)
    sine = (-jnp.sin(angle)).astype(bf16).reshape(nlon, n_dev, own)
    table = jnp.stack([cosine, sine], axis=2)
    factor = jnp.where(flat_orders == 0, 1.0, 2.0).astype(bf16).reshape(n_dev, own)

    own_leg = jnp.pad(legendre, ((0, pad), (0, 0), (0, 0)))
    own_leg = lax.dynamic_slice_in_dim(own_leg, lon_pos * own, own)
    own_orders = lax.dynamic_slice_in_dim(orders, lat_pos * n_lon + lon_pos, 1)[0]
    mask = jnp.arange(degrees, dtype=jnp.int32)[None, :] >= own_orders[:, None]
    masked = jnp.where(mask[:, None, :], own_leg, jnp.zeros((), bf16))
    gram = jnp.einsum("kal,kbl->kab", own_leg, masked, preferred_element_type=f32).astype(bf16)

    parts = field.reshape(n_lon, own_rows, lon_cols, channels)
    slabs = lax.all_to_all(parts, "lon", split_axis=0, concat_axis=0, tiled=True)
    slabs = slabs.transpose(1, 0, 2, 3).reshape(own_rows, nlon, channels)
    own_quad = lax.dynamic_slice_in_dim(quad_weight, lon_pos * own_rows, own_rows)
    spectrum = jnp.einsum(
        "ajc,jq->aqc", slabs, table.reshape(nlon, -1), preferred_element_type=f32
    )
    spectrum = (spectrum * (own_quad * (1.0 / nlon))[:, None, None]).astype(bf16)
    spectrum = spectrum.reshape(own_rows, n_dev, 2 * own, channels).transpose(1, 0, 2, 3)
    gathered = lax.all_to_all(spectrum, BOTH, split_axis=0, concat_axis=0, tiled=True)
    gathered = gathered.reshape(nlat, 2, own, channels)
    grid = jnp.einsum("kab,brkc->arkc", gram, gathered, preferred_element_type=f32).astype(bf16)
    grid = grid.reshape(n_dev, own_rows, 2 * own, channels)
    grid = lax.all_to_all(grid, BOTH, split_axis=0, concat_axis=0, tiled=True)
    grid = grid.transpose(1, 0, 2, 3).reshape(own_rows, n_dev * 2 * own, channels)
    grid = lax.all_gather(grid, "lon", axis=0, tiled=True)

    here = lax.dynamic_slice_in_dim(table, lon_pos * lon_cols, lon_cols)
    here = here * factor[None, :, None, :]
    turned = jnp.stack([here[:, :, 1], -here[:, :, 0]], axis=2)
    direct = here.reshape(lon_cols, -1)
    turned = turned.reshape(lon_cols, -1)
    waves = [
        jnp.einsum("jq,aqc->ajc", piece, grid, preferred_element_type=f32).astype(bf16)
        for piece in (direct, turned)
    ]

    rimmed = padded(field, (("lon", 1),), 1, True)
    extended = padded(rimmed, (("lat", 0),), lat_rows, False)
    picks = support_blocks[0] - lat_pos + 1
    onehot = (picks[:, None] == jnp.arange(3, dtype=jnp.int32)[None, :]).astype(f32)
    operator = (
        jnp.einsum("tasb,sq->taqb", filter_values.astype(f32), onehot)
        .reshape(3, lat_rows, 3 * lat_rows)
        .astype(bf16)
    )
    responses = []
    for tap in range(3):
        window = extended[:, tap : tap + lon_cols]
        responses.append(
            jnp.einsum("ab,boc->aoc", operator[tap], window, preferred_element_type=f32).astype(
                bf16
            )
        )
    sources = [v.reshape(-1, channels) for v in waves + responses]
    weights = [spectral_weight[0], spectral_weight[1]] + [disco_weight[t] for t in range(3)]
    pre_act = sum(
        jnp.dot(s, w, preferred_element_type=f32) for s, w in zip(sources, weights)
    ).reshape(lat_rows, lon_cols, channels)
    activated, pullback = jax.vjp(jax.nn.gelu, pre_act)
    output = (field.astype(f32) + activated).astype(bf16)
    (grad_pre,) = pullback(cotangent.astype(f32))
    flat_grad = grad_pre.astype(bf16).reshape(-1, channels)
    grads = jnp.concatenate([outer_sum(s, flat_grad) for s in sources], axis=0)
    grads = grads.astype(bf16).reshape(n_dev, -1, channels)
    terms = lax.all_to_all(grads, BOTH, split_axis=0, concat_axis=0, tiled=True)
    total = jnp.sum(terms.astype(f32), axis=0).astype(bf16)
    total = lax.all_gather(total, BOTH, axis=0, tiled=True).astype(f32)
    total = total.reshape(5, channels, channels)
    return (output, total[:2], total[2:])


def solution(mesh):
    placed = (
        P("lat", "lon", None),
        P("lat", "lon", None),
        P("lat", None, None),
        P("lat"),
        P(),
        P("lat", None),
        P(None, "lat", None, None),
        P(),
        P(),
    )
    return jax.shard_map(
        local,
        mesh=mesh,
        in_specs=placed,
        out_specs=(P("lat", "lon", None), P(), P()),
        check_vma=False,
    )
```

```python
import functools

import jax
import jax.numpy as jnp
from jax import lax
from jax.experimental import pallas as pl
from jax.experimental.pallas import tpu as pltpu
from jax.sharding import PartitionSpec as P

MESH = pl.DeviceIdType.MESH

BOTH = ("lat", "lon")


def padded(value, sides, width, wrap):
    for axis, dim in sides:
        size, length = (lax.axis_size(axis), value.shape[dim])
        up = [(i, (i + 1) % size) for i in range(size if wrap else size - 1)]
        down = [(j, i) for i, j in up]
        last = lax.slice_in_dim(value, length - width, length, axis=dim)
        leading = lax.slice_in_dim(value, 0, width, axis=dim)
        before = lax.ppermute(last, axis, up)
        after = lax.ppermute(leading, axis, down)
        value = jnp.concatenate([before, value, after], axis=dim)
    return value


def greet_all(n, n_lon, me):
    barrier = pltpu.get_barrier_semaphore()

    def signal(step, carry):
        d = lax.rem(me + step, n)
        pl.semaphore_signal(
            barrier, inc=1, device_id=(d // n_lon, lax.rem(d, n_lon)), device_id_type=MESH
        )
        return carry

    lax.fori_loop(1, n, signal, 0)
    pl.semaphore_wait(barrier, n - 1)


def push(src, dst, send_sem, recv_sem, d, n_lon):
    return pltpu.make_async_remote_copy(
        src_ref=src,
        dst_ref=dst,
        send_sem=send_sem,
        recv_sem=recv_sem,
        device_id=(d // n_lon, lax.rem(d, n_lon)),
        device_id_type=MESH,
    )


def reduce_kernel(n, n_lon, x_ref, out_ref, parts, total, gath, s1, r1, s2, r2):
    me = lax.axis_index("lat") * n_lon + lax.axis_index("lon")
    greet_all(n, n_lon, me)

    def scatter(step, carry):
        d = lax.rem(me + step, n)
        push(x_ref.at[d], parts.at[me], s1.at[d], r1.at[me], d, n_lon).start()
        return carry

    lax.fori_loop(1, n, scatter, 0)

    def add(step, acc):
        d = lax.rem(me + n - step, n)
        push(x_ref.at[d], parts.at[d], s1.at[d], r1.at[d], d, n_lon).wait_recv()
        return acc + parts[d].astype(jnp.float32)

    total[...] = lax.fori_loop(1, n, add, x_ref[me].astype(jnp.float32)).astype(total.dtype)

    def spread(step, carry):
        d = lax.rem(me + step, n)
        push(total, gath.at[me], s2.at[d], r2.at[me], d, n_lon).start()
        return carry

    lax.fori_loop(1, n, spread, 0)
    out_ref[me] = total[...].astype(out_ref.dtype)

    def collect(step, carry):
        d = lax.rem(me + n - step, n)
        push(total, gath.at[d], s2.at[d], r2.at[d], d, n_lon).wait_recv()
        out_ref[d] = gath[d].astype(out_ref.dtype)
        return carry

    lax.fori_loop(1, n, collect, 0)

    def drain(step, carry):
        d = lax.rem(me + step, n)
        push(x_ref.at[d], parts.at[me], s1.at[d], r1.at[me], d, n_lon).wait_send()
        push(total, gath.at[me], s2.at[d], r2.at[me], d, n_lon).wait_send()
        return carry

    lax.fori_loop(1, n, drain, 0)


def reduce_all(values, n, n_lon):
    size = values.size
    rows = -(-size // (128 * n * 16)) * 16
    flat = jnp.pad(values.reshape(-1), (0, rows * 128 * n - size)).reshape(n, rows, 128)
    vmem = pl.BlockSpec(memory_space=pltpu.VMEM)
    dma = pltpu.SemaphoreType.DMA((n,))
    out = pl.pallas_call(
        functools.partial(reduce_kernel, n, n_lon),
        out_shape=jax.ShapeDtypeStruct((n, rows, 128), jnp.float32),
        in_specs=[vmem],
        out_specs=vmem,
        scratch_shapes=[
            pltpu.VMEM((n, rows, 128), jnp.bfloat16),
            pltpu.VMEM((rows, 128), jnp.bfloat16),
            pltpu.VMEM((n, rows, 128), jnp.bfloat16),
            dma,
            dma,
            dma,
            dma,
        ],
        compiler_params=pltpu.CompilerParams(
            collective_id=0, has_side_effects=True, vmem_limit_bytes=32 * 2**20
        ),
    )(flat.astype(jnp.bfloat16))
    return out.reshape(-1)[:size].reshape(values.shape)


def outer_sum(left, right):
    return lax.dot_general(
        left, right, (((0,), (0,)), ((), ())), preferred_element_type=jnp.float32
    )


def local(
    field,
    cotangent,
    legendre,
    quad_weight,
    order_slots,
    support_blocks,
    filter_values,
    spectral_weight,
    disco_weight,
):
    f32 = jnp.float32
    bf16 = jnp.bfloat16
    lat_rows, lon_cols, channels = field.shape
    n_lon = lax.axis_size("lon")
    n_dev = n_lon * lax.axis_size("lat")
    nlon = lon_cols * n_lon
    slots_dev, nlat, degrees = legendre.shape
    own_rows = lat_rows // n_lon
    lat_pos = lax.axis_index("lat")
    lon_pos = lax.axis_index("lon")
    own = -(-slots_dev // n_lon)
    pad = own * n_lon - slots_dev

    orders = order_slots.reshape(-1, slots_dev)
    orders = jnp.pad(orders, ((0, 0), (0, pad))).reshape(n_dev, own)
    flat_orders = orders.reshape(-1)
    column = jnp.arange(nlon, dtype=jnp.int32)
    phase = column[:, None] * flat_orders[None, :] % nlon
    angle = phase.astype(f32) * (2.0 * jnp.pi / nlon)
    cosine = jnp.cos(angle).astype(bf16).reshape(nlon, n_dev, own)
    sine = (-jnp.sin(angle)).astype(bf16).reshape(nlon, n_dev, own)
    table = jnp.stack([cosine, sine], axis=2)
    factor = jnp.where(flat_orders == 0, 1.0, 2.0).astype(bf16).reshape(n_dev, own)

    own_leg = jnp.pad(legendre, ((0, pad), (0, 0), (0, 0)))
    own_leg = lax.dynamic_slice_in_dim(own_leg, lon_pos * own, own)
    own_orders = lax.dynamic_slice_in_dim(orders, lat_pos * n_lon + lon_pos, 1)[0]
    mask = jnp.arange(degrees, dtype=jnp.int32)[None, :] >= own_orders[:, None]
    masked = jnp.where(mask[:, None, :], own_leg, jnp.zeros((), bf16))
    gram = jnp.einsum("kal,kbl->kab", own_leg, masked, preferred_element_type=f32).astype(bf16)

    parts = field.reshape(n_lon, own_rows, lon_cols, channels)
    slabs = lax.all_to_all(parts, "lon", split_axis=0, concat_axis=0, tiled=True)
    slabs = slabs.transpose(1, 0, 2, 3).reshape(own_rows, nlon, channels)
    own_quad = lax.dynamic_slice_in_dim(quad_weight, lon_pos * own_rows, own_rows)
    spectrum = jnp.einsum(
        "ajc,jq->aqc", slabs, table.reshape(nlon, -1), preferred_element_type=f32
    )
    spectrum = (spectrum * (own_quad * (1.0 / nlon))[:, None, None]).astype(bf16)
    spectrum = spectrum.reshape(own_rows, n_dev, 2 * own, channels).transpose(1, 0, 2, 3)
    gathered = lax.all_to_all(spectrum, BOTH, split_axis=0, concat_axis=0, tiled=True)
    gathered = gathered.reshape(nlat, 2, own, channels)
    grid = jnp.einsum("kab,brkc->arkc", gram, gathered, preferred_element_type=f32).astype(bf16)
    grid = grid.reshape(n_dev, own_rows, 2 * own, channels)
    grid = lax.all_to_all(grid, BOTH, split_axis=0, concat_axis=0, tiled=True)
    grid = grid.transpose(1, 0, 2, 3).reshape(own_rows, n_dev * 2 * own, channels)
    grid = lax.all_gather(grid, "lon", axis=0, tiled=True)

    here = lax.dynamic_slice_in_dim(table, lon_pos * lon_cols, lon_cols)
    here = here * factor[None, :, None, :]
    turned = jnp.stack([here[:, :, 1], -here[:, :, 0]], axis=2)
    direct = here.reshape(lon_cols, -1)
    turned = turned.reshape(lon_cols, -1)
    waves = [
        jnp.einsum("jq,aqc->ajc", piece, grid, preferred_element_type=f32).astype(bf16)
        for piece in (direct, turned)
    ]

    rimmed = padded(field, (("lon", 1),), 1, True)
    extended = padded(rimmed, (("lat", 0),), lat_rows, False)
    picks = support_blocks[0] - lat_pos + 1
    onehot = (picks[:, None] == jnp.arange(3, dtype=jnp.int32)[None, :]).astype(f32)
    operator = (
        jnp.einsum("tasb,sq->taqb", filter_values.astype(f32), onehot)
        .reshape(3, lat_rows, 3 * lat_rows)
        .astype(bf16)
    )
    responses = []
    for tap in range(3):
        window = extended[:, tap : tap + lon_cols]
        responses.append(
            jnp.einsum("ab,boc->aoc", operator[tap], window, preferred_element_type=f32).astype(
                bf16
            )
        )
    sources = [v.reshape(-1, channels) for v in waves + responses]
    weights = [spectral_weight[0], spectral_weight[1]] + [disco_weight[t] for t in range(3)]
    pre_act = sum(
        jnp.dot(s, w, preferred_element_type=f32) for s, w in zip(sources, weights)
    ).reshape(lat_rows, lon_cols, channels)
    activated, pullback = jax.vjp(jax.nn.gelu, pre_act)
    output = (field.astype(f32) + activated).astype(bf16)
    (grad_pre,) = pullback(cotangent.astype(f32))
    flat_grad = grad_pre.astype(bf16).reshape(-1, channels)
    grads = jnp.concatenate([outer_sum(s, flat_grad) for s in sources], axis=0)
    total = reduce_all(grads.reshape(5, channels, channels), n_dev, n_lon)
    return (output, total[:2], total[2:])


def solution(mesh):
    placed = (
        P("lat", "lon", None),
        P("lat", "lon", None),
        P("lat", None, None),
        P("lat"),
        P(),
        P("lat", None),
        P(None, "lat", None, None),
        P(),
        P(),
    )
    return jax.shard_map(
        local,
        mesh=mesh,
        in_specs=placed,
        out_specs=(P("lat", "lon", None), P(), P()),
        check_vma=False,
    )
```

```python
import functools

import jax
import jax.numpy as jnp
from jax import lax
from jax.experimental import pallas as pl
from jax.experimental.pallas import tpu as pltpu
from jax.sharding import PartitionSpec as P

MESH = pl.DeviceIdType.MESH

BOTH = ("lat", "lon")


def padded(value, sides, width, wrap):
    for axis, dim in sides:
        size, length = (lax.axis_size(axis), value.shape[dim])
        up = [(i, (i + 1) % size) for i in range(size if wrap else size - 1)]
        down = [(j, i) for i, j in up]
        last = lax.slice_in_dim(value, length - width, length, axis=dim)
        leading = lax.slice_in_dim(value, 0, width, axis=dim)
        before = lax.ppermute(last, axis, up)
        after = lax.ppermute(leading, axis, down)
        value = jnp.concatenate([before, value, after], axis=dim)
    return value


def greet_all(n, n_lon, me):
    barrier = pltpu.get_barrier_semaphore()

    def signal(step, carry):
        d = lax.rem(me + step, n)
        pl.semaphore_signal(
            barrier, inc=1, device_id=(d // n_lon, lax.rem(d, n_lon)), device_id_type=MESH
        )
        return carry

    lax.fori_loop(1, n, signal, 0)
    pl.semaphore_wait(barrier, n - 1)


def push(src, dst, send_sem, recv_sem, d, n_lon):
    return pltpu.make_async_remote_copy(
        src_ref=src,
        dst_ref=dst,
        send_sem=send_sem,
        recv_sem=recv_sem,
        device_id=(d // n_lon, lax.rem(d, n_lon)),
        device_id_type=MESH,
    )


def reduce_kernel(n, n_lon, x_ref, out_ref, parts, total, gath, s1, r1, s2, r2):
    me = lax.axis_index("lat") * n_lon + lax.axis_index("lon")
    greet_all(n, n_lon, me)

    def scatter(step, carry):
        d = lax.rem(me + step, n)
        push(x_ref.at[d], parts.at[me], s1.at[d], r1.at[me], d, n_lon).start()
        return carry

    lax.fori_loop(1, n, scatter, 0)

    def add(step, acc):
        d = lax.rem(me + n - step, n)
        push(x_ref.at[d], parts.at[d], s1.at[d], r1.at[d], d, n_lon).wait_recv()
        return acc + parts[d].astype(jnp.float32)

    total[...] = lax.fori_loop(1, n, add, x_ref[me].astype(jnp.float32)).astype(total.dtype)

    def spread(step, carry):
        d = lax.rem(me + step, n)
        push(total, gath.at[me], s2.at[d], r2.at[me], d, n_lon).start()
        return carry

    lax.fori_loop(1, n, spread, 0)
    out_ref[me] = total[...].astype(out_ref.dtype)

    def collect(step, carry):
        d = lax.rem(me + n - step, n)
        push(total, gath.at[d], s2.at[d], r2.at[d], d, n_lon).wait_recv()
        out_ref[d] = gath[d].astype(out_ref.dtype)
        return carry

    lax.fori_loop(1, n, collect, 0)

    def drain(step, carry):
        d = lax.rem(me + step, n)
        push(x_ref.at[d], parts.at[me], s1.at[d], r1.at[me], d, n_lon).wait_send()
        push(total, gath.at[me], s2.at[d], r2.at[me], d, n_lon).wait_send()
        return carry

    lax.fori_loop(1, n, drain, 0)


def reduce_all(values, n, n_lon):
    size = values.size
    rows = -(-size // (128 * n * 16)) * 16
    flat = jnp.pad(values.reshape(-1), (0, rows * 128 * n - size)).reshape(n, rows, 128)
    vmem = pl.BlockSpec(memory_space=pltpu.VMEM)
    dma = pltpu.SemaphoreType.DMA((n,))
    out = pl.pallas_call(
        functools.partial(reduce_kernel, n, n_lon),
        out_shape=jax.ShapeDtypeStruct((n, rows, 128), jnp.float32),
        in_specs=[vmem],
        out_specs=vmem,
        scratch_shapes=[
            pltpu.VMEM((n, rows, 128), jnp.bfloat16),
            pltpu.VMEM((rows, 128), jnp.bfloat16),
            pltpu.VMEM((n, rows, 128), jnp.bfloat16),
            dma,
            dma,
            dma,
            dma,
        ],
        compiler_params=pltpu.CompilerParams(
            collective_id=0, has_side_effects=True, vmem_limit_bytes=32 * 2**20
        ),
    )(flat.astype(jnp.bfloat16))
    return out.reshape(-1)[:size].reshape(values.shape)


def spectral_kernel(
    n_lat,
    n_lon,
    own_rows,
    field_ref,
    rim_ref,
    cols_ref,
    leg_ref,
    q_ref,
    halo_ref,
    tab_ref,
    slab,
    table,
    spec,
    gram,
    same,
    msg,
    recv,
    grid,
    back,
    own_sem,
    s_lon,
    r_lon,
    s_out,
    r_out,
    s_back,
    r_back,
    s_q,
    r_q,
    s_halo,
    r_halo,
):
    f32 = jnp.float32
    bf16 = jnp.bfloat16
    lat = lax.axis_index("lat")
    lon = lax.axis_index("lon")
    n = n_lat * n_lon
    me = lat * n_lon + lon
    rows = msg.shape[1]
    part = rows // own_rows
    band = slab.shape[1]
    lon_cols = band // own_rows
    nlon = lon_cols * n_lon
    greet_all(n, n_lon, me)

    up = push(rim_ref, halo_ref.at[0], s_halo.at[0], r_halo.at[0], me + n_lon, n_lon)
    down = push(rim_ref, halo_ref.at[1], s_halo.at[1], r_halo.at[1], me - n_lon, n_lon)

    def to_lon(t):
        src = field_ref.at[pl.ds(pl.multiple_of(t * band, 16), band)]
        return push(src, slab.at[lon], s_lon.at[t], r_lon.at[lon], lat * n_lon + t, n_lon)

    for step in range(n_lon - 1, 0, -1):
        to_lon(lax.rem(lon + step, n_lon)).start()

    @pl.when(lat < n_lat - 1)
    def _():
        up.start()

    @pl.when(lat > 0)
    def _():
        down.start()

    slab[lon] = field_ref[pl.ds(pl.multiple_of(lon * band, 16), band)]

    chunk = 64

    def tables(i, carry):
        at = pl.ds(pl.multiple_of(i * chunk, chunk), chunk)
        order = cols_ref[at, 0:1]
        shift = cols_ref[at, 1:2]
        j = lax.broadcasted_iota(jnp.int32, (chunk, lon_cols), 1).astype(f32)
        for s in range(n_lon):
            turn = (j + float(s * lon_cols)) * order + shift
            turn = turn - jnp.round(turn * (1.0 / nlon)) * float(nlon)
            x = (0.25 - jnp.abs(turn) * (1.0 / nlon)) * 6.283185307179586
            y = x * x
            p = -2.505210838544172e-8
            for c in (2.7557319223985893e-6, -1.984126984126984e-4, 8.333333333333333e-3, -0.16666666666666666, 1.0):
                p = p * y + c
            table[s, at] = (p * x).astype(bf16)
        return carry

    lax.fori_loop(0, table.shape[1] // chunk, tables, 0)
    tab_ref[...] = table[lon]

    total = gram.shape[0]
    block = same.shape[0]
    kind = lax.rem(lax.broadcasted_iota(jnp.int32, (block, total), 0), part)
    other = lax.rem(lax.broadcasted_iota(jnp.int32, (block, total), 1), part)
    same[...] = jnp.where(kind == other, 1.0, 0.0)

    def grams(i, carry):
        at = pl.ds(pl.multiple_of(i * block, 16), block)
        product = lax.dot_general(
            leg_ref[at], leg_ref[...], (((1,), (1,)), ((), ())), preferred_element_type=f32
        )
        gram[at] = (product * same[...]).astype(bf16)
        return carry

    lax.fori_loop(0, total // block, grams, 0)

    for step in range(n_lon):
        s = lax.rem(lon + step, n_lon)
        if step:
            push(slab.at[s], slab.at[s], s_lon.at[s], r_lon.at[s], me, n_lon).wait_recv()
        wide = slab[s].astype(f32)
        for a in range(own_rows):
            piece = wide[a * lon_cols : (a + 1) * lon_cols].astype(bf16)
            term = jnp.dot(table[s], piece, preferred_element_type=f32)
            if step:
                term = term + spec[a]
            if step == n_lon - 1:
                term = term * cols_ref[:, 2 + a : 3 + a]
            spec[a] = term

    def message(d):
        at = pl.ds(pl.multiple_of(d * part, 8), part)
        return jnp.concatenate([spec[a, at] for a in range(own_rows)], axis=0).astype(bf16)

    def to_owner(d):
        return push(msg.at[d], recv.at[me], s_out.at[d], r_out.at[me], d, n_lon)

    def send_out(step, carry):
        d = lax.rem(me + step, n)
        msg[d] = message(d)
        to_owner(d).start()
        return carry

    lax.fori_loop(1, n, send_out, 0)
    recv[me] = message(me)

    def await_out(step, carry):
        d = lax.rem(me + n - step, n)
        push(msg.at[d], recv.at[d], s_out.at[d], r_out.at[d], d, n_lon).wait_recv()
        return carry

    lax.fori_loop(1, n, await_out, 0)

    per = block // rows
    blocks = total // block

    def to_rows(d):
        return push(grid.at[d], back.at[me], s_back.at[d], r_back.at[me], d, n_lon)

    def send_back(i, carry):
        b = lax.rem(me // per + 1 + i, blocks)
        at = pl.ds(pl.multiple_of(b * block, 16), block)
        value = jnp.dot(
            gram[at], recv[...].reshape(total, recv.shape[2]), preferred_element_type=f32
        ).astype(bf16)
        for e in range(per):
            d = b * per + e
            grid[d] = value[e * rows : (e + 1) * rows]

            @pl.when(d != me)
            def _():
                to_rows(d).start()

        return carry

    lax.fori_loop(0, blocks, send_back, 0)
    back[me] = grid[me]

    def await_back(step, carry):
        d = lax.rem(me + n - step, n)
        push(grid.at[d], back.at[d], s_back.at[d], r_back.at[d], d, n_lon).wait_recv()
        return carry

    lax.fori_loop(1, n, await_back, 0)

    def to_slab(t):
        return push(back, q_ref.at[lon], s_q.at[t], r_q.at[lon], lat * n_lon + t, n_lon)

    keep = pltpu.make_async_copy(back, q_ref.at[lon], own_sem)
    keep.start()
    half = n_lon // 2
    side = lax.rem(lon, half)
    cross = lax.rem(lon + half, n_lon)
    if n_lon == 4:
        mate = lon - side + (1 - side)
        far = lax.rem(mate + half, n_lon)
        to_slab(cross).start()
        to_slab(mate).start()
        push(back, q_ref.at[cross], s_q.at[cross], r_q.at[cross], me, n_lon).wait_recv()
        relay = push(
            q_ref.at[cross], q_ref.at[cross], s_q.at[far], r_q.at[n_lon], lat * n_lon + mate, n_lon
        )
        relay.start()
        push(back, q_ref.at[mate], s_q.at[mate], r_q.at[mate], me, n_lon).wait_recv()
        push(back, q_ref.at[far], s_q.at[far], r_q.at[n_lon], me, n_lon).wait_recv()
        to_slab(cross).wait_send()
        to_slab(mate).wait_send()
        relay.wait_send()
    else:
        for step in range(1, n_lon):
            to_slab(lax.rem(lon + step, n_lon)).start()
        for step in range(1, n_lon):
            t = lax.rem(lon + step, n_lon)
            push(back, q_ref.at[t], s_q.at[t], r_q.at[t], me, n_lon).wait_recv()
            to_slab(t).wait_send()
    keep.wait()

    for step in range(1, n_lon):
        to_lon(lax.rem(lon + step, n_lon)).wait_send()

    def drain(step, carry):
        d = lax.rem(me + step, n)
        to_owner(d).wait_send()
        to_rows(d).wait_send()
        return carry

    lax.fori_loop(1, n, drain, 0)

    @pl.when(lat < n_lat - 1)
    def _():
        up.wait_send()
        down.wait_recv()

    @pl.when(lat > 0)
    def _():
        down.wait_send()
        up.wait_recv()


def spectral(field, rimmed, cols, leg, n_lat, n_lon, own_rows):
    lat_rows, lon_cols, channels = field.shape
    n = n_lat * n_lon
    total = leg.shape[0]
    rows = total // n
    bf16 = jnp.bfloat16
    f32 = jnp.float32
    band = own_rows * lon_cols
    q_rows = cols.shape[0]
    block = total // 8
    vmem = pl.BlockSpec(memory_space=pltpu.VMEM)
    anywhere = pl.BlockSpec(memory_space=pl.ANY)
    dma = pltpu.SemaphoreType.DMA
    flat_rim = rimmed.reshape(-1, channels)
    return pl.pallas_call(
        functools.partial(spectral_kernel, n_lat, n_lon, own_rows),
        out_shape=(
            jax.ShapeDtypeStruct((n_lon, n, rows, channels), bf16),
            jax.ShapeDtypeStruct((2,) + flat_rim.shape, bf16),
            jax.ShapeDtypeStruct((q_rows, lon_cols), bf16),
        ),
        in_specs=[vmem, anywhere, vmem, vmem],
        out_specs=(anywhere, anywhere, vmem),
        scratch_shapes=[
            pltpu.VMEM((n_lon, band, channels), bf16),
            pltpu.VMEM((n_lon, q_rows, lon_cols), bf16),
            pltpu.VMEM((own_rows, q_rows, channels), f32),
            pltpu.VMEM((total, total), bf16),
            pltpu.VMEM((block, total), f32),
        ]
        + [pltpu.VMEM((n, rows, channels), bf16)] * 4
        + [dma]
        + [dma((n_lon,))] * 2
        + [dma((n,))] * 4
        + [dma((n_lon,)), dma((n_lon + 1,))]
        + [dma((2,))] * 2,
        compiler_params=pltpu.CompilerParams(
            collective_id=1, has_side_effects=True, vmem_limit_bytes=52 * 2**20
        ),
    )(field.reshape(-1, channels), flat_rim, cols, leg)


def outer_sum(left, right):
    return lax.dot_general(
        left, right, (((0,), (0,)), ((), ())), preferred_element_type=jnp.float32
    )


def local(
    field,
    cotangent,
    legendre,
    quad_weight,
    order_slots,
    support_blocks,
    filter_values,
    spectral_weight,
    disco_weight,
):
    f32 = jnp.float32
    bf16 = jnp.bfloat16
    lat_rows, lon_cols, channels = field.shape
    n_lon = lax.axis_size("lon")
    n_dev = n_lon * lax.axis_size("lat")
    nlon = lon_cols * n_lon
    slots_dev, nlat, degrees = legendre.shape
    own_rows = lat_rows // n_lon
    lat_pos = lax.axis_index("lat")
    lon_pos = lax.axis_index("lon")
    own = -(-slots_dev // n_lon)
    pad = own * n_lon - slots_dev

    orders = order_slots.reshape(-1, slots_dev)
    orders = jnp.pad(orders, ((0, 0), (0, pad))).reshape(n_dev, own)
    flat_orders = orders.reshape(-1)
    own_leg = jnp.pad(legendre, ((0, pad), (0, 0), (0, 0)))
    own_leg = lax.dynamic_slice_in_dim(own_leg, lon_pos * own, own)
    own_orders = lax.dynamic_slice_in_dim(orders, lat_pos * n_lon + lon_pos, 1)[0]
    mask = jnp.arange(degrees, dtype=jnp.int32)[None, :] >= own_orders[:, None]
    masked = jnp.where(mask[:, None, :], own_leg, jnp.zeros((), bf16))
    own_quad = lax.dynamic_slice_in_dim(quad_weight, lon_pos * own_rows, own_rows)
    rimmed = padded(field, (("lon", 1),), 1, True)
    if own % 4 == 0 and n_dev * own % 64 == 0 and own_rows * lon_cols % 16 == 0:
        shape = (n_dev, 2, own)
        factor = jnp.where(orders == 0, 1.0, 2.0)[:, None, :] / nlon
        cols = [
            jnp.broadcast_to(orders[:, None, :].astype(f32), shape),
            jnp.broadcast_to(jnp.array([0.0, nlon / 4], f32)[None, :, None], shape),
        ]
        cols += [jnp.broadcast_to(factor * own_quad[a], shape) for a in range(own_rows)]
        cols = jnp.stack([c.reshape(-1) for c in cols], axis=1)
        leg = jnp.broadcast_to(
            masked.transpose(1, 0, 2)[:, None], (nlat, 2, own, degrees)
        ).reshape(-1, degrees)
        grid, halo, direct = spectral(field, rimmed, cols, leg, lax.axis_size("lat"), n_lon, own_rows)
        grid = grid.reshape(n_lon, n_dev, own_rows, 2 * own, channels)
        grid = grid.transpose(0, 2, 1, 3, 4).reshape(lat_rows, -1, channels)
        pair = direct.reshape(n_dev, 2, own, lon_cols)
        turned = jnp.stack([pair[:, 1], -pair[:, 0]], axis=1).reshape(-1, lon_cols)
        waves = [
            jnp.einsum("qj,aqc->ajc", piece, grid, preferred_element_type=f32).astype(bf16)
            for piece in (direct, turned)
        ]
        halo = halo.reshape(2, lat_rows, lon_cols + 2, channels)
        zero = jnp.zeros((), bf16)
        extended = jnp.concatenate(
            [
                jnp.where(lat_pos > 0, halo[0], zero),
                rimmed,
                jnp.where(lat_pos < lax.axis_size("lat") - 1, halo[1], zero),
            ],
            axis=0,
        )
    else:
        column = jnp.arange(nlon, dtype=jnp.int32)
        phase = column[:, None] * flat_orders[None, :] % nlon
        angle = phase.astype(f32) * (2.0 * jnp.pi / nlon)
        cosine = jnp.cos(angle).astype(bf16).reshape(nlon, n_dev, own)
        sine = (-jnp.sin(angle)).astype(bf16).reshape(nlon, n_dev, own)
        table = jnp.stack([cosine, sine], axis=2)
        factor = jnp.where(flat_orders == 0, 1.0, 2.0).astype(bf16).reshape(n_dev, own)
        gram = jnp.einsum("kal,kbl->kab", own_leg, masked, preferred_element_type=f32).astype(bf16)

        parts = field.reshape(n_lon, own_rows, lon_cols, channels)
        slabs = lax.all_to_all(parts, "lon", split_axis=0, concat_axis=0, tiled=True)
        slabs = slabs.transpose(1, 0, 2, 3).reshape(own_rows, nlon, channels)
        spectrum = jnp.einsum(
            "ajc,jq->aqc", slabs, table.reshape(nlon, -1), preferred_element_type=f32
        )
        spectrum = (spectrum * (own_quad * (1.0 / nlon))[:, None, None]).astype(bf16)
        spectrum = spectrum.reshape(own_rows, n_dev, 2 * own, channels).transpose(1, 0, 2, 3)
        gathered = lax.all_to_all(spectrum, BOTH, split_axis=0, concat_axis=0, tiled=True)
        gathered = gathered.reshape(nlat, 2, own, channels)
        grid = jnp.einsum("kab,brkc->arkc", gram, gathered, preferred_element_type=f32).astype(bf16)
        grid = grid.reshape(n_dev, own_rows, 2 * own, channels)
        grid = lax.all_to_all(grid, BOTH, split_axis=0, concat_axis=0, tiled=True)
        grid = grid.transpose(1, 0, 2, 3).reshape(own_rows, n_dev * 2 * own, channels)
        grid = lax.all_gather(grid, "lon", axis=0, tiled=True)

        here = lax.dynamic_slice_in_dim(table, lon_pos * lon_cols, lon_cols)
        here = here * factor[None, :, None, :]
        turned = jnp.stack([here[:, :, 1], -here[:, :, 0]], axis=2)
        direct = here.reshape(lon_cols, -1)
        turned = turned.reshape(lon_cols, -1)
        waves = [
            jnp.einsum("jq,aqc->ajc", piece, grid, preferred_element_type=f32).astype(bf16)
            for piece in (direct, turned)
        ]
        extended = padded(rimmed, (("lat", 0),), lat_rows, False)

    picks = support_blocks[0] - lat_pos + 1
    onehot = (picks[:, None] == jnp.arange(3, dtype=jnp.int32)[None, :]).astype(f32)
    operator = (
        jnp.einsum("tasb,sq->taqb", filter_values.astype(f32), onehot)
        .reshape(3, lat_rows, 3 * lat_rows)
        .astype(bf16)
    )
    responses = []
    for tap in range(3):
        window = extended[:, tap : tap + lon_cols]
        responses.append(
            jnp.einsum("ab,boc->aoc", operator[tap], window, preferred_element_type=f32).astype(
                bf16
            )
        )
    sources = [v.reshape(-1, channels) for v in waves + responses]
    weights = [spectral_weight[0], spectral_weight[1]] + [disco_weight[t] for t in range(3)]
    pre_act = sum(
        jnp.dot(s, w, preferred_element_type=f32) for s, w in zip(sources, weights)
    ).reshape(lat_rows, lon_cols, channels)
    activated, pullback = jax.vjp(jax.nn.gelu, pre_act)
    output = (field.astype(f32) + activated).astype(bf16)
    (grad_pre,) = pullback(cotangent.astype(f32))
    flat_grad = grad_pre.astype(bf16).reshape(-1, channels)
    grads = jnp.concatenate([outer_sum(s, flat_grad) for s in sources], axis=0)
    total = reduce_all(grads.reshape(5, channels, channels), n_dev, n_lon)
    return (output, total[:2], total[2:])


def solution(mesh):
    placed = (
        P("lat", "lon", None),
        P("lat", "lon", None),
        P("lat", None, None),
        P("lat"),
        P(),
        P("lat", None),
        P(None, "lat", None, None),
        P(),
        P(),
    )
    return jax.shard_map(
        local,
        mesh=mesh,
        in_specs=placed,
        out_specs=(P("lat", "lon", None), P(), P()),
        check_vma=False,
    )
```

```python
import functools

import jax
import jax.numpy as jnp
from jax import lax
from jax.experimental import pallas as pl
from jax.experimental.pallas import tpu as pltpu
from jax.sharding import PartitionSpec as P

MESH = pl.DeviceIdType.MESH

BOTH = ("lat", "lon")


def padded(value, sides, width, wrap):
    for axis, dim in sides:
        size, length = (lax.axis_size(axis), value.shape[dim])
        up = [(i, (i + 1) % size) for i in range(size if wrap else size - 1)]
        down = [(j, i) for i, j in up]
        last = lax.slice_in_dim(value, length - width, length, axis=dim)
        leading = lax.slice_in_dim(value, 0, width, axis=dim)
        before = lax.ppermute(last, axis, up)
        after = lax.ppermute(leading, axis, down)
        value = jnp.concatenate([before, value, after], axis=dim)
    return value


def greet_all(n, n_lon, me):
    barrier = pltpu.get_barrier_semaphore()

    def signal(step, carry):
        d = lax.rem(me + step, n)
        pl.semaphore_signal(
            barrier, inc=1, device_id=(d // n_lon, lax.rem(d, n_lon)), device_id_type=MESH
        )
        return carry

    lax.fori_loop(1, n, signal, 0)
    pl.semaphore_wait(barrier, n - 1)


def push(src, dst, send_sem, recv_sem, d, n_lon):
    return pltpu.make_async_remote_copy(
        src_ref=src,
        dst_ref=dst,
        send_sem=send_sem,
        recv_sem=recv_sem,
        device_id=(d // n_lon, lax.rem(d, n_lon)),
        device_id_type=MESH,
    )


def reduce_kernel(
    n_lat, n_lon, x_ref, out_ref, half, pair, parts, total, gath, s0, r0, s1, r1, s2, r2, s3, r3
):
    f32 = jnp.float32
    lat = lax.axis_index("lat")
    lon = lax.axis_index("lon")
    side = lax.rem(lon, 2)
    mate = lon + 1 - 2 * side
    wide = n_lon // 2
    n = n_lat * wide
    me = lat * wide + lon // 2

    def place(g):
        return (g // wide, lax.rem(g, wide) * 2 + side)

    barrier = pltpu.get_barrier_semaphore()
    pl.semaphore_signal(barrier, inc=1, device_id=(lat, mate), device_id_type=MESH)

    def signal(step, carry):
        pl.semaphore_signal(
            barrier, inc=1, device_id=place(lax.rem(me + step, n)), device_id_type=MESH
        )
        return carry

    lax.fori_loop(1, n, signal, 0)
    pl.semaphore_wait(barrier, n)

    def copy(src, dst, send_sem, recv_sem, where):
        return pltpu.make_async_remote_copy(
            src_ref=src,
            dst_ref=dst,
            send_sem=send_sem,
            recv_sem=recv_sem,
            device_id=where,
            device_id_type=MESH,
        )

    first = copy(x_ref.at[1 - side], half, s0, r0, (lat, mate))
    first.start()
    first.wait()

    def scatter(step, carry):
        g = lax.rem(me + step, n)
        pair[g] = (x_ref[side, g].astype(f32) + half[g].astype(f32)).astype(pair.dtype)
        copy(pair.at[g], parts.at[me], s1.at[g], r1.at[me], place(g)).start()
        return carry

    lax.fori_loop(1, n, scatter, 0)

    def add(step, acc):
        g = lax.rem(me + n - step, n)
        copy(pair.at[g], parts.at[g], s1.at[g], r1.at[g], place(g)).wait_recv()
        return acc + parts[g].astype(f32)

    own = x_ref[side, me].astype(f32) + half[me].astype(f32)
    total[...] = lax.fori_loop(1, n, add, own).astype(total.dtype)

    def spread(step, carry):
        g = lax.rem(me + step, n)
        copy(total, gath.at[side, me], s2.at[g], r2.at[me], place(g)).start()
        return carry

    lax.fori_loop(1, n, spread, 0)
    gath[side, me] = total[...]

    def collect(step, carry):
        g = lax.rem(me + n - step, n)
        copy(total, gath.at[side, g], s2.at[g], r2.at[g], place(g)).wait_recv()
        return carry

    lax.fori_loop(1, n, collect, 0)
    last = copy(gath.at[side], gath.at[side], s3, r3, (lat, mate))
    last.start()
    out_ref[side] = gath[side].astype(f32)
    last.wait_send()
    copy(gath.at[1 - side], gath.at[1 - side], s3, r3, (lat, mate)).wait_recv()
    out_ref[1 - side] = gath[1 - side].astype(f32)

    def drain(step, carry):
        g = lax.rem(me + step, n)
        copy(pair.at[g], parts.at[me], s1.at[g], r1.at[me], place(g)).wait_send()
        copy(total, gath.at[side, me], s2.at[g], r2.at[me], place(g)).wait_send()
        return carry

    lax.fori_loop(1, n, drain, 0)


def reduce_all(values, n_lat, n_lon):
    size = values.size
    n = n_lat * n_lon // 2
    rows = -(-size // (128 * 2 * n * 16)) * 16
    flat = jnp.pad(values.reshape(-1), (0, rows * 256 * n - size)).reshape(2, n, rows, 128)
    vmem = pl.BlockSpec(memory_space=pltpu.VMEM)
    dma = pltpu.SemaphoreType.DMA
    slots = pltpu.VMEM((n, rows, 128), jnp.bfloat16)
    out = pl.pallas_call(
        functools.partial(reduce_kernel, n_lat, n_lon),
        out_shape=jax.ShapeDtypeStruct((2, n, rows, 128), jnp.float32),
        in_specs=[vmem],
        out_specs=vmem,
        scratch_shapes=[
            slots,
            slots,
            slots,
            pltpu.VMEM((rows, 128), jnp.bfloat16),
            pltpu.VMEM((2, n, rows, 128), jnp.bfloat16),
            dma,
            dma,
        ]
        + [dma((n,))] * 4
        + [dma, dma],
        compiler_params=pltpu.CompilerParams(
            collective_id=0, has_side_effects=True, vmem_limit_bytes=32 * 2**20
        ),
    )(flat.astype(jnp.bfloat16))
    return out.reshape(-1)[:size].reshape(values.shape)


def spectral_kernel(
    n_lat,
    n_lon,
    own_rows,
    field_ref,
    rim_ref,
    cols_ref,
    leg_ref,
    q_ref,
    halo_ref,
    tab_ref,
    slab,
    table,
    spec,
    gram,
    same,
    msg,
    recv,
    grid,
    back,
    pack,
    legs,
    own_sem,
    s_lon,
    r_lon,
    s_out,
    r_out,
    s_back,
    r_back,
    s_q,
    r_q,
    s_halo,
    r_halo,
):
    f32 = jnp.float32
    bf16 = jnp.bfloat16
    lat = lax.axis_index("lat")
    lon = lax.axis_index("lon")
    n = n_lat * n_lon
    me = lat * n_lon + lon
    rows = msg.shape[1]
    part = rows // own_rows
    band = slab.shape[1]
    lon_cols = band // own_rows
    nlon = lon_cols * n_lon
    greet_all(n, n_lon, me)

    odd = lax.rem(lat, 2)
    sign = 1 - 2 * odd
    hand_to = lat + 2 * sign
    has_other = jnp.logical_and(hand_to >= 0, hand_to < n_lat)
    from_other = lat - 2 * sign
    gets_other = jnp.logical_and(from_other >= 0, from_other < n_lat)
    cut = rim_ref.shape[0] // 32 * 16

    def piece_of(c):
        return pl.ds(cut, rim_ref.shape[0] - cut) if c else pl.ds(0, cut)

    def to_mate(c):
        at = piece_of(c)
        return push(
            rim_ref.at[at],
            halo_ref.at[odd, at],
            s_halo.at[c],
            r_halo.at[c],
            (lat + sign) * n_lon + lon,
            n_lon,
        )

    def got_mate(c):
        at = piece_of(c)
        dst = halo_ref.at[1 - odd, at]
        return push(dst, dst, s_halo.at[c], r_halo.at[c], me, n_lon)

    def hand_on(c):
        at = piece_of(c)
        return push(
            halo_ref.at[1 - odd, at],
            halo_ref.at[odd, at],
            s_halo.at[2 + c],
            r_halo.at[2 + c],
            hand_to * n_lon + lon,
            n_lon,
        )

    def relay_halo(c):
        got_mate(c).wait_recv()

        @pl.when(has_other)
        def _():
            hand_on(c).start()

    def to_lon(t):
        src = field_ref.at[pl.ds(pl.multiple_of(t * band, 16), band)]
        return push(src, slab.at[lon], s_lon.at[t], r_lon.at[lon], lat * n_lon + t, n_lon)

    for step in range(n_lon - 1, 0, -1):
        to_lon(lax.rem(lon + step, n_lon)).start()

    to_mate(0).start()
    slab[lon] = field_ref[pl.ds(pl.multiple_of(lon * band, 16), band)]

    chunk = 64

    def tables(i, carry):
        at = pl.ds(pl.multiple_of(i * chunk, chunk), chunk)
        order = cols_ref[at, 0:1]
        shift = cols_ref[at, 1:2]
        j = lax.broadcasted_iota(jnp.int32, (chunk, lon_cols), 1).astype(f32)
        for s in range(n_lon):
            turn = (j + float(s * lon_cols)) * order + shift
            turn = turn - jnp.round(turn * (1.0 / nlon)) * float(nlon)
            x = (0.25 - jnp.abs(turn) * (1.0 / nlon)) * 6.283185307179586
            y = x * x
            p = -2.505210838544172e-8
            for c in (2.7557319223985893e-6, -1.984126984126984e-4, 8.333333333333333e-3, -0.16666666666666666, 1.0):
                p = p * y + c
            table[s, at] = (p * x).astype(bf16)
        return carry

    lax.fori_loop(0, table.shape[1] // chunk, tables, 0)
    tab_ref[...] = table[lon]
    relay_halo(0)
    to_mate(1).start()

    total = gram.shape[0]
    block = same.shape[0]
    kind = lax.rem(lax.broadcasted_iota(jnp.int32, (block, total), 0), part)
    other = lax.rem(lax.broadcasted_iota(jnp.int32, (block, total), 1), part)
    same[...] = jnp.where(kind == other, 1.0, 0.0)

    nlat = n_lat * own_rows * n_lon
    own = part // 2

    def spread_rows(i, carry):
        at = pl.ds(pl.multiple_of(i * block, 16), block)
        row = i * block + lax.broadcasted_iota(jnp.int32, (block, 1), 0)
        wanted = lax.rem(row, own) * nlat + lax.div(row, part)
        column = lax.broadcasted_iota(jnp.int32, (block, leg_ref.shape[0]), 1)
        pick = jnp.where(column == wanted, 1.0, 0.0).astype(bf16)
        legs[at] = jnp.dot(pick, leg_ref[...], preferred_element_type=f32).astype(bf16)
        return carry

    lax.fori_loop(0, total // block, spread_rows, 0)

    def grams(i, carry):
        at = pl.ds(pl.multiple_of(i * block, 16), block)
        product = lax.dot_general(
            legs[at], legs[...], (((1,), (1,)), ((), ())), preferred_element_type=f32
        )
        gram[at] = (product * same[...]).astype(bf16)
        return carry

    lax.fori_loop(0, total // block, grams, 0)

    for step in range(n_lon):
        s = lax.rem(lon + step, n_lon)
        if step:
            push(slab.at[s], slab.at[s], s_lon.at[s], r_lon.at[s], me, n_lon).wait_recv()
        wide = slab[s].astype(f32)
        for a in range(own_rows):
            piece = wide[a * lon_cols : (a + 1) * lon_cols].astype(bf16)
            term = jnp.dot(table[s], piece, preferred_element_type=f32)
            if step:
                term = term + spec[a]
            if step == n_lon - 1:
                term = term * cols_ref[:, 2 + a : 3 + a]
            spec[a] = term

    def message(d):
        at = pl.ds(pl.multiple_of(d * part, 8), part)
        return jnp.concatenate([spec[a, at] for a in range(own_rows)], axis=0).astype(bf16)

    def to_owner(d):
        return push(msg.at[d], recv.at[me], s_out.at[d], r_out.at[me], d, n_lon)

    def send_out(step, carry):
        d = lax.rem(me + step, n)
        msg[d] = message(d)
        to_owner(d).start()
        return carry

    lax.fori_loop(1, n, send_out, 0)
    recv[me] = message(me)

    def await_out(step, carry):
        d = lax.rem(me + n - step, n)
        push(msg.at[d], recv.at[d], s_out.at[d], r_out.at[d], d, n_lon).wait_recv()
        return carry

    lax.fori_loop(1, n, await_out, 0)

    per = block // rows
    blocks = total // block

    def to_rows(d):
        return push(grid.at[d], back.at[me], s_back.at[d], r_back.at[me], d, n_lon)

    def send_back(i, carry):
        b = lax.rem(me // per + 1 + i, blocks)
        at = pl.ds(pl.multiple_of(b * block, 16), block)
        value = jnp.dot(
            gram[at], recv[...].reshape(total, recv.shape[2]), preferred_element_type=f32
        ).astype(bf16)
        for e in range(per):
            d = b * per + e
            grid[d] = value[e * rows : (e + 1) * rows]

            @pl.when(d != me)
            def _():
                to_rows(d).start()

        return carry

    lax.fori_loop(0, blocks, send_back, 0)
    back[me] = grid[me]

    def await_back(step, carry):
        d = lax.rem(me + n - step, n)
        push(grid.at[d], back.at[d], s_back.at[d], r_back.at[d], d, n_lon).wait_recv()
        return carry

    lax.fori_loop(1, n, await_back, 0)

    relay_halo(1)
    for a in range(own_rows):
        wide = back[:, a * part : (a + 1) * part].astype(f32)
        pack[a] = wide.reshape(pack.shape[1:]).astype(bf16)

    def to_slab(t):
        return push(pack, q_ref.at[lon], s_q.at[t], r_q.at[lon], lat * n_lon + t, n_lon)

    keep = pltpu.make_async_copy(pack, q_ref.at[lon], own_sem)
    keep.start()
    half = n_lon // 2
    side = lax.rem(lon, half)
    cross = lax.rem(lon + half, n_lon)
    if n_lon == 4:
        mate = lon - side + (1 - side)
        far = lax.rem(mate + half, n_lon)
        to_slab(cross).start()
        to_slab(mate).start()
        push(pack, q_ref.at[cross], s_q.at[cross], r_q.at[cross], me, n_lon).wait_recv()
        relay = push(
            q_ref.at[cross], q_ref.at[cross], s_q.at[far], r_q.at[n_lon], lat * n_lon + mate, n_lon
        )
        relay.start()
        push(pack, q_ref.at[mate], s_q.at[mate], r_q.at[mate], me, n_lon).wait_recv()
        push(pack, q_ref.at[far], s_q.at[far], r_q.at[n_lon], me, n_lon).wait_recv()
        to_slab(cross).wait_send()
        to_slab(mate).wait_send()
        relay.wait_send()
    else:
        for step in range(1, n_lon):
            to_slab(lax.rem(lon + step, n_lon)).start()
        for step in range(1, n_lon):
            t = lax.rem(lon + step, n_lon)
            push(pack, q_ref.at[t], s_q.at[t], r_q.at[t], me, n_lon).wait_recv()
            to_slab(t).wait_send()
    keep.wait()

    for step in range(1, n_lon):
        to_lon(lax.rem(lon + step, n_lon)).wait_send()

    def drain(step, carry):
        d = lax.rem(me + step, n)
        to_owner(d).wait_send()
        to_rows(d).wait_send()
        return carry

    lax.fori_loop(1, n, drain, 0)

    for c in range(2):
        to_mate(c).wait_send()

        @pl.when(has_other)
        def _():
            hand_on(c).wait_send()

        @pl.when(gets_other)
        def _():
            dst = halo_ref.at[odd, piece_of(c)]
            push(dst, dst, s_halo.at[2 + c], r_halo.at[2 + c], me, n_lon).wait_recv()


def spectral(field, rimmed, cols, leg, n_lat, n_lon, own_rows):
    lat_rows, lon_cols, channels = field.shape
    n = n_lat * n_lon
    total = 2 * leg.shape[0]
    rows = total // n
    bf16 = jnp.bfloat16
    f32 = jnp.float32
    band = own_rows * lon_cols
    q_rows = cols.shape[0]
    block = total // 8
    vmem = pl.BlockSpec(memory_space=pltpu.VMEM)
    anywhere = pl.BlockSpec(memory_space=pl.ANY)
    dma = pltpu.SemaphoreType.DMA
    flat_rim = rimmed.reshape(-1, channels)
    return pl.pallas_call(
        functools.partial(spectral_kernel, n_lat, n_lon, own_rows),
        out_shape=(
            jax.ShapeDtypeStruct((n_lon, own_rows, q_rows, channels), bf16),
            jax.ShapeDtypeStruct((2,) + flat_rim.shape, bf16),
            jax.ShapeDtypeStruct((q_rows, lon_cols), bf16),
        ),
        in_specs=[vmem, anywhere, vmem, vmem],
        out_specs=(anywhere, anywhere, vmem),
        scratch_shapes=[
            pltpu.VMEM((n_lon, band, channels), bf16),
            pltpu.VMEM((n_lon, q_rows, lon_cols), bf16),
            pltpu.VMEM((own_rows, q_rows, channels), f32),
            pltpu.VMEM((total, total), bf16),
            pltpu.VMEM((block, total), f32),
        ]
        + [pltpu.VMEM((n, rows, channels), bf16)] * 4
        + [pltpu.VMEM((own_rows, q_rows, channels), bf16), pltpu.VMEM((total, leg.shape[1]), bf16)]
        + [dma]
        + [dma((n_lon,))] * 2
        + [dma((n,))] * 4
        + [dma((n_lon,)), dma((n_lon + 1,))]
        + [dma((4,))] * 2,
        compiler_params=pltpu.CompilerParams(
            collective_id=1, has_side_effects=True, vmem_limit_bytes=52 * 2**20
        ),
    )(field.reshape(-1, channels), flat_rim, cols, leg)


def outer_sum(left, right):
    return lax.dot_general(
        left, right, (((0,), (0,)), ((), ())), preferred_element_type=jnp.float32
    )


def local(
    field,
    cotangent,
    legendre,
    quad_weight,
    order_slots,
    support_blocks,
    filter_values,
    spectral_weight,
    disco_weight,
):
    f32 = jnp.float32
    bf16 = jnp.bfloat16
    lat_rows, lon_cols, channels = field.shape
    n_lon = lax.axis_size("lon")
    n_dev = n_lon * lax.axis_size("lat")
    nlon = lon_cols * n_lon
    slots_dev, nlat, degrees = legendre.shape
    own_rows = lat_rows // n_lon
    lat_pos = lax.axis_index("lat")
    lon_pos = lax.axis_index("lon")
    own = -(-slots_dev // n_lon)
    pad = own * n_lon - slots_dev

    orders = order_slots.reshape(-1, slots_dev)
    orders = jnp.pad(orders, ((0, 0), (0, pad))).reshape(n_dev, own)
    flat_orders = orders.reshape(-1)
    own_leg = jnp.pad(legendre, ((0, pad), (0, 0), (0, 0)))
    own_leg = lax.dynamic_slice_in_dim(own_leg, lon_pos * own, own)
    own_orders = lax.dynamic_slice_in_dim(orders, lat_pos * n_lon + lon_pos, 1)[0]
    mask = jnp.arange(degrees, dtype=jnp.int32)[None, :] >= own_orders[:, None]
    masked = jnp.where(mask[:, None, :], own_leg, jnp.zeros((), bf16))
    own_quad = lax.dynamic_slice_in_dim(quad_weight, lon_pos * own_rows, own_rows)
    rimmed = padded(field, (("lon", 1),), 1, True)
    if own % 4 == 0 and n_dev * own % 64 == 0 and own_rows * lon_cols % 16 == 0:
        shape = (n_dev, 2, own)
        factor = jnp.where(orders == 0, 1.0, 2.0)[:, None, :] / nlon
        cols = [
            jnp.broadcast_to(orders[:, None, :].astype(f32), shape),
            jnp.broadcast_to(jnp.array([0.0, nlon / 4], f32)[None, :, None], shape),
        ]
        cols += [jnp.broadcast_to(factor * own_quad[a], shape) for a in range(own_rows)]
        cols = jnp.stack([c.reshape(-1) for c in cols], axis=1)
        leg = masked.reshape(-1, degrees)
        grid, halo, direct = spectral(field, rimmed, cols, leg, lax.axis_size("lat"), n_lon, own_rows)
        grid = grid.reshape(lat_rows, -1, channels)
        pair = direct.reshape(n_dev, 2, own, lon_cols)
        turned = jnp.stack([pair[:, 1], -pair[:, 0]], axis=1).reshape(-1, lon_cols)
        waves = [
            jnp.einsum("qj,aqc->ajc", piece, grid, preferred_element_type=f32).astype(bf16)
            for piece in (direct, turned)
        ]
        halo = halo.reshape(2, lat_rows, lon_cols + 2, channels)
        zero = jnp.zeros((), bf16)
        extended = jnp.concatenate(
            [
                jnp.where(lat_pos > 0, halo[0], zero),
                rimmed,
                jnp.where(lat_pos < lax.axis_size("lat") - 1, halo[1], zero),
            ],
            axis=0,
        )
    else:
        column = jnp.arange(nlon, dtype=jnp.int32)
        phase = column[:, None] * flat_orders[None, :] % nlon
        angle = phase.astype(f32) * (2.0 * jnp.pi / nlon)
        cosine = jnp.cos(angle).astype(bf16).reshape(nlon, n_dev, own)
        sine = (-jnp.sin(angle)).astype(bf16).reshape(nlon, n_dev, own)
        table = jnp.stack([cosine, sine], axis=2)
        factor = jnp.where(flat_orders == 0, 1.0, 2.0).astype(bf16).reshape(n_dev, own)
        gram = jnp.einsum("kal,kbl->kab", own_leg, masked, preferred_element_type=f32).astype(bf16)

        parts = field.reshape(n_lon, own_rows, lon_cols, channels)
        slabs = lax.all_to_all(parts, "lon", split_axis=0, concat_axis=0, tiled=True)
        slabs = slabs.transpose(1, 0, 2, 3).reshape(own_rows, nlon, channels)
        spectrum = jnp.einsum(
            "ajc,jq->aqc", slabs, table.reshape(nlon, -1), preferred_element_type=f32
        )
        spectrum = (spectrum * (own_quad * (1.0 / nlon))[:, None, None]).astype(bf16)
        spectrum = spectrum.reshape(own_rows, n_dev, 2 * own, channels).transpose(1, 0, 2, 3)
        gathered = lax.all_to_all(spectrum, BOTH, split_axis=0, concat_axis=0, tiled=True)
        gathered = gathered.reshape(nlat, 2, own, channels)
        grid = jnp.einsum("kab,brkc->arkc", gram, gathered, preferred_element_type=f32).astype(bf16)
        grid = grid.reshape(n_dev, own_rows, 2 * own, channels)
        grid = lax.all_to_all(grid, BOTH, split_axis=0, concat_axis=0, tiled=True)
        grid = grid.transpose(1, 0, 2, 3).reshape(own_rows, n_dev * 2 * own, channels)
        grid = lax.all_gather(grid, "lon", axis=0, tiled=True)

        here = lax.dynamic_slice_in_dim(table, lon_pos * lon_cols, lon_cols)
        here = here * factor[None, :, None, :]
        turned = jnp.stack([here[:, :, 1], -here[:, :, 0]], axis=2)
        direct = here.reshape(lon_cols, -1)
        turned = turned.reshape(lon_cols, -1)
        waves = [
            jnp.einsum("jq,aqc->ajc", piece, grid, preferred_element_type=f32).astype(bf16)
            for piece in (direct, turned)
        ]
        extended = padded(rimmed, (("lat", 0),), lat_rows, False)

    picks = support_blocks[0] - lat_pos + 1
    onehot = (picks[:, None] == jnp.arange(3, dtype=jnp.int32)[None, :]).astype(f32)
    operator = (
        jnp.einsum("tasb,sq->taqb", filter_values.astype(f32), onehot)
        .reshape(3, lat_rows, 3 * lat_rows)
        .astype(bf16)
    )
    responses = []
    for tap in range(3):
        window = extended[:, tap : tap + lon_cols]
        responses.append(
            jnp.einsum("ab,boc->aoc", operator[tap], window, preferred_element_type=f32).astype(
                bf16
            )
        )
    sources = [v.reshape(-1, channels) for v in waves + responses]
    weights = [spectral_weight[0], spectral_weight[1]] + [disco_weight[t] for t in range(3)]
    pre_act = sum(
        jnp.dot(s, w, preferred_element_type=f32) for s, w in zip(sources, weights)
    ).reshape(lat_rows, lon_cols, channels)
    activated, pullback = jax.vjp(jax.nn.gelu, pre_act)
    output = (field.astype(f32) + activated).astype(bf16)
    (grad_pre,) = pullback(cotangent.astype(f32))
    flat_grad = grad_pre.astype(bf16).reshape(-1, channels)
    grads = jnp.concatenate([outer_sum(s, flat_grad) for s in sources], axis=0)
    total = reduce_all(grads.reshape(5, channels, channels), lax.axis_size("lat"), n_lon)
    return (output, total[:2], total[2:])


def solution(mesh):
    placed = (
        P("lat", "lon", None),
        P("lat", "lon", None),
        P("lat", None, None),
        P("lat"),
        P(),
        P("lat", None),
        P(None, "lat", None, None),
        P(),
        P(),
    )
    return jax.shard_map(
        local,
        mesh=mesh,
        in_specs=placed,
        out_specs=(P("lat", "lon", None), P(), P()),
        check_vma=False,
    )
```

```python
import functools

import jax
import jax.numpy as jnp
from jax import lax
from jax.experimental import pallas as pl
from jax.experimental.pallas import tpu as pltpu
from jax.sharding import PartitionSpec as P

MESH = pl.DeviceIdType.MESH
SINE = (2.7557319223985893e-6, -1.984126984126984e-4, 8.333333333333333e-3, -1 / 6, 1.0)

BOTH = ("lat", "lon")


def padded(value, sides, width, wrap):
    for axis, dim in sides:
        size, length = (lax.axis_size(axis), value.shape[dim])
        up = [(i, (i + 1) % size) for i in range(size if wrap else size - 1)]
        down = [(j, i) for i, j in up]
        last = lax.slice_in_dim(value, length - width, length, axis=dim)
        leading = lax.slice_in_dim(value, 0, width, axis=dim)
        before = lax.ppermute(last, axis, up)
        after = lax.ppermute(leading, axis, down)
        value = jnp.concatenate([before, value, after], axis=dim)
    return value


def greet_all(n, n_lon, me):
    barrier = pltpu.get_barrier_semaphore()

    def signal(step, carry):
        d = lax.rem(me + step, n)
        pl.semaphore_signal(
            barrier, inc=1, device_id=(d // n_lon, lax.rem(d, n_lon)), device_id_type=MESH
        )
        return carry

    lax.fori_loop(1, n, signal, 0)
    pl.semaphore_wait(barrier, n - 1)


def push(src, dst, send_sem, recv_sem, d, n_lon):
    return pltpu.make_async_remote_copy(
        src_ref=src,
        dst_ref=dst,
        send_sem=send_sem,
        recv_sem=recv_sem,
        device_id=(d // n_lon, lax.rem(d, n_lon)),
        device_id_type=MESH,
    )


def reduce_kernel(
    n_lat, n_lon, x_ref, out_ref, half, pair, parts, total, gath, s0, r0, s1, r1, s2, r2, s3, r3
):
    f32 = jnp.float32
    lat = lax.axis_index("lat")
    lon = lax.axis_index("lon")
    side = lax.rem(lon, 2)
    mate = lon + 1 - 2 * side
    wide = n_lon // 2
    n = n_lat * wide
    me = lat * wide + lon // 2

    def place(g):
        return (g // wide, lax.rem(g, wide) * 2 + side)

    barrier = pltpu.get_barrier_semaphore()
    pl.semaphore_signal(barrier, inc=1, device_id=(lat, mate), device_id_type=MESH)

    def signal(step, carry):
        pl.semaphore_signal(
            barrier, inc=1, device_id=place(lax.rem(me + step, n)), device_id_type=MESH
        )
        return carry

    lax.fori_loop(1, n, signal, 0)
    pl.semaphore_wait(barrier, n)

    def copy(src, dst, send_sem, recv_sem, where):
        return pltpu.make_async_remote_copy(
            src_ref=src,
            dst_ref=dst,
            send_sem=send_sem,
            recv_sem=recv_sem,
            device_id=where,
            device_id_type=MESH,
        )

    first = copy(x_ref.at[1 - side], half, s0, r0, (lat, mate))
    first.start()
    first.wait()

    def scatter(step, carry):
        g = lax.rem(me + step, n)
        pair[g] = (x_ref[side, g].astype(f32) + half[g].astype(f32)).astype(pair.dtype)
        copy(pair.at[g], parts.at[me], s1.at[g], r1.at[me], place(g)).start()
        return carry

    lax.fori_loop(1, n, scatter, 0)

    def add(step, acc):
        g = lax.rem(me + n - step, n)
        copy(pair.at[g], parts.at[g], s1.at[g], r1.at[g], place(g)).wait_recv()
        return acc + parts[g].astype(f32)

    own = x_ref[side, me].astype(f32) + half[me].astype(f32)
    total[...] = lax.fori_loop(1, n, add, own).astype(total.dtype)

    def spread(step, carry):
        g = lax.rem(me + step, n)
        copy(total, gath.at[side, me], s2.at[g], r2.at[me], place(g)).start()
        return carry

    lax.fori_loop(1, n, spread, 0)
    gath[side, me] = total[...]

    def collect(step, carry):
        g = lax.rem(me + n - step, n)
        copy(total, gath.at[side, g], s2.at[g], r2.at[g], place(g)).wait_recv()
        return carry

    lax.fori_loop(1, n, collect, 0)
    last = copy(gath.at[side], gath.at[side], s3, r3, (lat, mate))
    last.start()
    out_ref[side] = gath[side].astype(f32)
    last.wait_send()
    copy(gath.at[1 - side], gath.at[1 - side], s3, r3, (lat, mate)).wait_recv()
    out_ref[1 - side] = gath[1 - side].astype(f32)

    def drain(step, carry):
        g = lax.rem(me + step, n)
        copy(pair.at[g], parts.at[me], s1.at[g], r1.at[me], place(g)).wait_send()
        copy(total, gath.at[side, me], s2.at[g], r2.at[me], place(g)).wait_send()
        return carry

    lax.fori_loop(1, n, drain, 0)


def reduce_all(values, n_lat, n_lon):
    size = values.size
    n = n_lat * n_lon // 2
    rows = -(-size // (128 * 2 * n * 16)) * 16
    flat = jnp.pad(values.reshape(-1), (0, rows * 256 * n - size)).reshape(2, n, rows, 128)
    vmem = pl.BlockSpec(memory_space=pltpu.VMEM)
    dma = pltpu.SemaphoreType.DMA
    slots = pltpu.VMEM((n, rows, 128), jnp.bfloat16)
    out = pl.pallas_call(
        functools.partial(reduce_kernel, n_lat, n_lon),
        out_shape=jax.ShapeDtypeStruct((2, n, rows, 128), jnp.float32),
        in_specs=[vmem],
        out_specs=vmem,
        scratch_shapes=[
            slots,
            slots,
            slots,
            pltpu.VMEM((rows, 128), jnp.bfloat16),
            pltpu.VMEM((2, n, rows, 128), jnp.bfloat16),
            dma,
            dma,
        ]
        + [dma((n,))] * 4
        + [dma, dma],
        compiler_params=pltpu.CompilerParams(
            collective_id=0, has_side_effects=True, vmem_limit_bytes=32 * 2**20
        ),
    )(flat.astype(jnp.bfloat16))
    return out.reshape(-1)[:size].reshape(values.shape)


def spectral_kernel(
    n_lat,
    n_lon,
    own_rows,
    field_ref,
    rim_ref,
    cols_ref,
    leg_ref,
    q_ref,
    ext_ref,
    tab_ref,
    slab,
    table,
    spec,
    gram,
    same,
    msg,
    recv,
    grid,
    back,
    pack,
    legs,
    zeros,
    own_sem,
    s_lon,
    r_lon,
    s_out,
    r_out,
    s_back,
    r_back,
    s_q,
    r_q,
    s_halo,
    r_halo,
):
    f32 = jnp.float32
    bf16 = jnp.bfloat16
    lat = lax.axis_index("lat")
    lon = lax.axis_index("lon")
    n = n_lat * n_lon
    me = lat * n_lon + lon
    rows = msg.shape[1]
    part = rows // own_rows
    band = slab.shape[1]
    lon_cols = band // own_rows
    nlon = lon_cols * n_lon
    greet_all(n, n_lon, me)

    odd = lax.rem(lat, 2)
    sign = 1 - 2 * odd
    hand_to = lat + 2 * sign
    has_other = jnp.logical_and(hand_to >= 0, hand_to < n_lat)
    from_other = lat - 2 * sign
    gets_other = jnp.logical_and(from_other >= 0, from_other < n_lat)
    cut = rim_ref.shape[0] // 32 * 16

    def piece_of(c):
        return pl.ds(cut, rim_ref.shape[0] - cut) if c else pl.ds(0, cut)

    def to_mate(c):
        at = piece_of(c)
        return push(
            rim_ref.at[at],
            ext_ref.at[2 * odd, at],
            s_halo.at[c],
            r_halo.at[c],
            (lat + sign) * n_lon + lon,
            n_lon,
        )

    def got_mate(c):
        at = piece_of(c)
        dst = ext_ref.at[2 - 2 * odd, at]
        return push(dst, dst, s_halo.at[c], r_halo.at[c], me, n_lon)

    def hand_on(c):
        at = piece_of(c)
        return push(
            ext_ref.at[2 - 2 * odd, at],
            ext_ref.at[2 * odd, at],
            s_halo.at[2 + c],
            r_halo.at[2 + c],
            hand_to * n_lon + lon,
            n_lon,
        )

    def relay_halo(c):
        got_mate(c).wait_recv()

        @pl.when(has_other)
        def _():
            hand_on(c).start()

    def to_lon(t):
        src = field_ref.at[pl.ds(pl.multiple_of(t * band, 16), band)]
        return push(src, slab.at[lon], s_lon.at[t], r_lon.at[lon], lat * n_lon + t, n_lon)

    for step in range(n_lon - 1, 0, -1):
        to_lon(lax.rem(lon + step, n_lon)).start()

    to_mate(0).start()
    own_block = pltpu.make_async_copy(rim_ref, ext_ref.at[1], own_sem.at[1])
    own_block.start()
    blank = pltpu.make_async_copy(zeros, ext_ref.at[2 * odd], own_sem.at[2])

    @pl.when(jnp.logical_not(gets_other))
    def _():
        zeros[...] = jnp.zeros_like(zeros)
        blank.start()

    slab[lon] = field_ref[pl.ds(pl.multiple_of(lon * band, 16), band)]

    chunk = 64

    def wave(phase):
        turn = phase - jnp.round(phase * (1.0 / nlon)) * float(nlon)
        x = (0.25 - jnp.abs(turn) * (1.0 / nlon)) * 6.283185307179586
        y = x * x
        p = -2.505210838544172e-8
        for c in SINE:
            p = p * y + c
        return (p * x).astype(bf16)

    def tables(i, carry):
        at = pl.ds(pl.multiple_of(i * chunk, chunk), chunk)
        order = cols_ref[at, 0:1]
        shift = cols_ref[at, 1:2]
        j = lax.broadcasted_iota(jnp.int32, (chunk, lon_cols), 1).astype(f32)
        for s in range(n_lon):
            table[s, at] = wave((j + float(s * lon_cols)) * order + shift)
        tab_ref[1, at] = wave((j + (lon * lon_cols).astype(f32)) * order + (shift + nlon / 4.0))
        return carry

    lax.fori_loop(0, table.shape[1] // chunk, tables, 0)
    tab_ref[0] = table[lon]
    relay_halo(0)
    to_mate(1).start()

    for step in range(n_lon):
        s = lax.rem(lon + step, n_lon)
        if step:
            push(slab.at[s], slab.at[s], s_lon.at[s], r_lon.at[s], me, n_lon).wait_recv()
        wide = slab[s].astype(f32)
        for a in range(own_rows):
            piece = wide[a * lon_cols : (a + 1) * lon_cols].astype(bf16)
            term = jnp.dot(table[s], piece, preferred_element_type=f32)
            if step:
                term = term + spec[a]
            if step == n_lon - 1:
                term = term * cols_ref[:, 2 + a : 3 + a]
            spec[a] = term

    def message(d):
        at = pl.ds(pl.multiple_of(d * part, 8), part)
        return jnp.concatenate([spec[a, at] for a in range(own_rows)], axis=0).astype(bf16)

    def to_owner(d):
        return push(msg.at[d], recv.at[me], s_out.at[d], r_out.at[me], d, n_lon)

    def send_out(step, carry):
        d = lax.rem(me + step, n)
        msg[d] = message(d)
        to_owner(d).start()
        return carry

    lax.fori_loop(1, n, send_out, 0)
    recv[me] = message(me)

    total = gram.shape[0]
    block = same.shape[0]
    kind = lax.rem(lax.broadcasted_iota(jnp.int32, (block, total), 0), part)
    other = lax.rem(lax.broadcasted_iota(jnp.int32, (block, total), 1), part)
    same[...] = jnp.where(kind == other, 1.0, 0.0)

    nlat = n_lat * own_rows * n_lon
    own = part // 2

    def spread_rows(i, carry):
        at = pl.ds(pl.multiple_of(i * block, 16), block)
        row = i * block + lax.broadcasted_iota(jnp.int32, (block, 1), 0)
        wanted = lax.rem(row, own) * nlat + lax.div(row, part)
        column = lax.broadcasted_iota(jnp.int32, (block, leg_ref.shape[0]), 1)
        pick = jnp.where(column == wanted, 1.0, 0.0).astype(bf16)
        legs[at] = jnp.dot(pick, leg_ref[...], preferred_element_type=f32).astype(bf16)
        return carry

    lax.fori_loop(0, total // block, spread_rows, 0)

    def grams(i, carry):
        at = pl.ds(pl.multiple_of(i * block, 16), block)
        product = lax.dot_general(
            legs[at], legs[...], (((1,), (1,)), ((), ())), preferred_element_type=f32
        )
        gram[at] = (product * same[...]).astype(bf16)
        return carry

    lax.fori_loop(0, total // block, grams, 0)

    def await_out(step, carry):
        d = lax.rem(me + n - step, n)
        push(msg.at[d], recv.at[d], s_out.at[d], r_out.at[d], d, n_lon).wait_recv()
        return carry

    lax.fori_loop(1, n, await_out, 0)

    per = block // rows
    blocks = total // block

    def to_rows(d):
        return push(grid.at[d], back.at[me], s_back.at[d], r_back.at[me], d, n_lon)

    def send_back(i, carry):
        b = lax.rem(me // per + 1 + i, blocks)
        at = pl.ds(pl.multiple_of(b * block, 16), block)
        value = jnp.dot(
            gram[at], recv[...].reshape(total, recv.shape[2]), preferred_element_type=f32
        ).astype(bf16)
        for e in range(per):
            d = b * per + e
            grid[d] = value[e * rows : (e + 1) * rows]

            @pl.when(d != me)
            def _():
                to_rows(d).start()

        return carry

    lax.fori_loop(0, blocks, send_back, 0)
    back[me] = grid[me]

    relay_halo(1)
    span = n_lon * part

    def group(i):
        g = lax.rem(lat + 2 * n_lat - 1 - i, n_lat)
        return g, pl.ds(pl.multiple_of(g * span, 16), span)

    def to_slab(t, g, at):
        return push(
            pack.at[:, at],
            q_ref.at[lon, :, at],
            s_q.at[t, g],
            r_q.at[lon, g],
            lat * n_lon + t,
            n_lon,
        )

    def got(t, g, at, slot):
        dst = q_ref.at[t, :, at]
        return push(dst, dst, s_q.at[t, g], r_q.at[slot, g], me, n_lon)

    half = n_lon // 2
    cross = lax.rem(lon + half, n_lon)
    side = lax.rem(lon, half)
    mate = lon - side + (half - 1 - side)
    far = lax.rem(mate + half, n_lon)
    paired = n_lon == 4
    targets = (cross, mate) if paired else [lax.rem(lon + e, n_lon) for e in range(1, n_lon)]

    def relay(g, at):
        dst = q_ref.at[cross, :, at]
        return push(dst, dst, s_q.at[far, g], r_q.at[n_lon, g], lat * n_lon + mate, n_lon)

    def gather(i, carry):
        g, at = group(i)
        for e in range(n_lon):
            d = g * n_lon + e

            @pl.when(d != me)
            def _():
                push(grid.at[d], back.at[d], s_back.at[d], r_back.at[d], d, n_lon).wait_recv()

        wide = back[pl.ds(g * n_lon, n_lon)].astype(f32)
        for a in range(own_rows):
            rows_a = wide[:, a * part : (a + 1) * part]
            pack[a, at] = rows_a.reshape(span, wide.shape[2]).astype(bf16)
        for t in targets:
            to_slab(t, g, at).start()
        return carry

    lax.fori_loop(0, n_lat, gather, 0)
    keep = pltpu.make_async_copy(pack, q_ref.at[lon], own_sem.at[0])
    keep.start()

    def hand_over(i, carry):
        g, at = group(i)
        got(cross, g, at, cross).wait_recv()
        relay(g, at).start()
        return carry

    def finish(i, carry):
        g, at = group(i)
        for t in targets:
            to_slab(t, g, at).wait_send()
        if paired:
            got(mate, g, at, mate).wait_recv()
            got(far, g, at, n_lon).wait_recv()
            relay(g, at).wait_send()
        else:
            for t in targets:
                got(t, g, at, t).wait_recv()
        return carry

    if paired:
        lax.fori_loop(0, n_lat, hand_over, 0)
    lax.fori_loop(0, n_lat, finish, 0)
    keep.wait()

    for step in range(1, n_lon):
        to_lon(lax.rem(lon + step, n_lon)).wait_send()

    def drain(step, carry):
        d = lax.rem(me + step, n)
        to_owner(d).wait_send()
        to_rows(d).wait_send()
        return carry

    lax.fori_loop(1, n, drain, 0)

    own_block.wait()

    @pl.when(jnp.logical_not(gets_other))
    def _():
        blank.wait()

    for c in range(2):
        to_mate(c).wait_send()

        @pl.when(has_other)
        def _():
            hand_on(c).wait_send()

        @pl.when(gets_other)
        def _():
            dst = ext_ref.at[2 * odd, piece_of(c)]
            push(dst, dst, s_halo.at[2 + c], r_halo.at[2 + c], me, n_lon).wait_recv()


def spectral(field, rimmed, cols, leg, n_lat, n_lon, own_rows):
    lat_rows, lon_cols, channels = field.shape
    n = n_lat * n_lon
    total = 2 * leg.shape[0]
    rows = total // n
    bf16 = jnp.bfloat16
    f32 = jnp.float32
    band = own_rows * lon_cols
    q_rows = cols.shape[0]
    block = total // 8
    vmem = pl.BlockSpec(memory_space=pltpu.VMEM)
    anywhere = pl.BlockSpec(memory_space=pl.ANY)
    dma = pltpu.SemaphoreType.DMA
    flat_rim = rimmed.reshape(-1, channels)
    return pl.pallas_call(
        functools.partial(spectral_kernel, n_lat, n_lon, own_rows),
        out_shape=(
            jax.ShapeDtypeStruct((n_lon, own_rows, q_rows, channels), bf16),
            jax.ShapeDtypeStruct((3,) + flat_rim.shape, bf16),
            jax.ShapeDtypeStruct((2, q_rows, lon_cols), bf16),
        ),
        in_specs=[vmem, anywhere, vmem, vmem],
        out_specs=(anywhere, anywhere, vmem),
        scratch_shapes=[
            pltpu.VMEM((n_lon, band, channels), bf16),
            pltpu.VMEM((n_lon, q_rows, lon_cols), bf16),
            pltpu.VMEM((own_rows, q_rows, channels), f32),
            pltpu.VMEM((total, total), bf16),
            pltpu.VMEM((block, total), f32),
        ]
        + [pltpu.VMEM((n, rows, channels), bf16)] * 4
        + [pltpu.VMEM((own_rows, q_rows, channels), bf16), pltpu.VMEM((total, leg.shape[1]), bf16)]
        + [pltpu.VMEM(flat_rim.shape, bf16), dma((3,))]
        + [dma((n_lon,))] * 2
        + [dma((n,))] * 4
        + [dma((n_lon, n_lat)), dma((n_lon + 1, n_lat))]
        + [dma((4,))] * 2,
        compiler_params=pltpu.CompilerParams(
            collective_id=1, has_side_effects=True, vmem_limit_bytes=52 * 2**20
        ),
    )(field.reshape(-1, channels), flat_rim, cols, leg)


def outer_sum(left, right):
    return lax.dot_general(
        left, right, (((0,), (0,)), ((), ())), preferred_element_type=jnp.float32
    )


def local(
    field,
    cotangent,
    legendre,
    quad_weight,
    order_slots,
    support_blocks,
    filter_values,
    spectral_weight,
    disco_weight,
):
    f32 = jnp.float32
    bf16 = jnp.bfloat16
    lat_rows, lon_cols, channels = field.shape
    n_lon = lax.axis_size("lon")
    n_dev = n_lon * lax.axis_size("lat")
    nlon = lon_cols * n_lon
    slots_dev, nlat, degrees = legendre.shape
    own_rows = lat_rows // n_lon
    lat_pos = lax.axis_index("lat")
    lon_pos = lax.axis_index("lon")
    own = -(-slots_dev // n_lon)
    pad = own * n_lon - slots_dev

    orders = order_slots.reshape(-1, slots_dev)
    orders = jnp.pad(orders, ((0, 0), (0, pad))).reshape(n_dev, own)
    flat_orders = orders.reshape(-1)
    own_leg = jnp.pad(legendre, ((0, pad), (0, 0), (0, 0)))
    own_leg = lax.dynamic_slice_in_dim(own_leg, lon_pos * own, own)
    own_orders = lax.dynamic_slice_in_dim(orders, lat_pos * n_lon + lon_pos, 1)[0]
    mask = jnp.arange(degrees, dtype=jnp.int32)[None, :] >= own_orders[:, None]
    masked = jnp.where(mask[:, None, :], own_leg, jnp.zeros((), bf16))
    own_quad = lax.dynamic_slice_in_dim(quad_weight, lon_pos * own_rows, own_rows)
    rimmed = padded(field, (("lon", 1),), 1, True)
    rimmed = jnp.pad(rimmed, ((0, 0), (0, -rimmed.shape[1] % 16), (0, 0)))
    if own % 4 == 0 and n_dev * own % 64 == 0 and own_rows * lon_cols % 16 == 0:
        shape = (n_dev, 2, own)
        factor = jnp.where(orders == 0, 1.0, 2.0)[:, None, :] / nlon
        cols = [
            jnp.broadcast_to(orders[:, None, :].astype(f32), shape),
            jnp.broadcast_to(jnp.array([0.0, nlon / 4], f32)[None, :, None], shape),
        ]
        cols += [jnp.broadcast_to(factor * own_quad[a], shape) for a in range(own_rows)]
        cols = jnp.stack([c.reshape(-1) for c in cols], axis=1)
        leg = masked.reshape(-1, degrees)
        grid, halo, direct = spectral(field, rimmed, cols, leg, lax.axis_size("lat"), n_lon, own_rows)
        grid = grid.reshape(lat_rows, -1, channels)
        waves = [
            jnp.einsum("qj,aqc->ajc", piece, grid, preferred_element_type=f32).astype(bf16)
            for piece in (direct[0], direct[1])
        ]
        extended = halo.reshape(3 * lat_rows, -1, channels)
    else:
        column = jnp.arange(nlon, dtype=jnp.int32)
        phase = column[:, None] * flat_orders[None, :] % nlon
        angle = phase.astype(f32) * (2.0 * jnp.pi / nlon)
        cosine = jnp.cos(angle).astype(bf16).reshape(nlon, n_dev, own)
        sine = (-jnp.sin(angle)).astype(bf16).reshape(nlon, n_dev, own)
        table = jnp.stack([cosine, sine], axis=2)
        factor = jnp.where(flat_orders == 0, 1.0, 2.0).astype(bf16).reshape(n_dev, own)
        gram = jnp.einsum("kal,kbl->kab", own_leg, masked, preferred_element_type=f32).astype(bf16)

        parts = field.reshape(n_lon, own_rows, lon_cols, channels)
        slabs = lax.all_to_all(parts, "lon", split_axis=0, concat_axis=0, tiled=True)
        slabs = slabs.transpose(1, 0, 2, 3).reshape(own_rows, nlon, channels)
        spectrum = jnp.einsum(
            "ajc,jq->aqc", slabs, table.reshape(nlon, -1), preferred_element_type=f32
        )
        spectrum = (spectrum * (own_quad * (1.0 / nlon))[:, None, None]).astype(bf16)
        spectrum = spectrum.reshape(own_rows, n_dev, 2 * own, channels).transpose(1, 0, 2, 3)
        gathered = lax.all_to_all(spectrum, BOTH, split_axis=0, concat_axis=0, tiled=True)
        gathered = gathered.reshape(nlat, 2, own, channels)
        grid = jnp.einsum("kab,brkc->arkc", gram, gathered, preferred_element_type=f32).astype(bf16)
        grid = grid.reshape(n_dev, own_rows, 2 * own, channels)
        grid = lax.all_to_all(grid, BOTH, split_axis=0, concat_axis=0, tiled=True)
        grid = grid.transpose(1, 0, 2, 3).reshape(own_rows, n_dev * 2 * own, channels)
        grid = lax.all_gather(grid, "lon", axis=0, tiled=True)

        here = lax.dynamic_slice_in_dim(table, lon_pos * lon_cols, lon_cols)
        here = here * factor[None, :, None, :]
        turned = jnp.stack([here[:, :, 1], -here[:, :, 0]], axis=2)
        direct = here.reshape(lon_cols, -1)
        turned = turned.reshape(lon_cols, -1)
        waves = [
            jnp.einsum("jq,aqc->ajc", piece, grid, preferred_element_type=f32).astype(bf16)
            for piece in (direct, turned)
        ]
        extended = padded(rimmed, (("lat", 0),), lat_rows, False)

    picks = support_blocks[0] - lat_pos + 1
    onehot = (picks[:, None] == jnp.arange(3, dtype=jnp.int32)[None, :]).astype(f32)
    operator = (
        jnp.einsum("tasb,sq->taqb", filter_values.astype(f32), onehot)
        .reshape(3, lat_rows, 3 * lat_rows)
        .astype(bf16)
    )
    responses = []
    for tap in range(3):
        window = extended[:, tap : tap + lon_cols]
        responses.append(
            jnp.einsum("ab,boc->aoc", operator[tap], window, preferred_element_type=f32).astype(
                bf16
            )
        )
    sources = [v.reshape(-1, channels) for v in waves + responses]
    weights = [spectral_weight[0], spectral_weight[1]] + [disco_weight[t] for t in range(3)]
    pre_act = sum(
        jnp.dot(s, w, preferred_element_type=f32) for s, w in zip(sources, weights)
    ).reshape(lat_rows, lon_cols, channels)
    activated, pullback = jax.vjp(jax.nn.gelu, pre_act)
    output = (field.astype(f32) + activated).astype(bf16)
    (grad_pre,) = pullback(cotangent.astype(f32))
    flat_grad = grad_pre.astype(bf16).reshape(-1, channels)
    grads = jnp.concatenate([outer_sum(s, flat_grad) for s in sources], axis=0)
    total = reduce_all(grads.reshape(5, channels, channels), lax.axis_size("lat"), n_lon)
    return (output, total[:2], total[2:])


def solution(mesh):
    placed = (
        P("lat", "lon", None),
        P("lat", "lon", None),
        P("lat", None, None),
        P("lat"),
        P(),
        P("lat", None),
        P(None, "lat", None, None),
        P(),
        P(),
    )
    return jax.shard_map(
        local,
        mesh=mesh,
        in_specs=placed,
        out_specs=(P("lat", "lon", None), P(), P()),
        check_vma=False,
    )
```

```python
import functools

import jax
import jax.numpy as jnp
from jax import lax
from jax.experimental import pallas as pl
from jax.experimental.pallas import tpu as pltpu
from jax.sharding import PartitionSpec as P

MESH = pl.DeviceIdType.MESH
PIECES = 4
SINE = (2.7557319223985893e-6, -1.984126984126984e-4, 8.333333333333333e-3, -1 / 6, 1.0)

BOTH = ("lat", "lon")


def padded(value, sides, width, wrap):
    for axis, dim in sides:
        size, length = (lax.axis_size(axis), value.shape[dim])
        up = [(i, (i + 1) % size) for i in range(size if wrap else size - 1)]
        down = [(j, i) for i, j in up]
        last = lax.slice_in_dim(value, length - width, length, axis=dim)
        leading = lax.slice_in_dim(value, 0, width, axis=dim)
        before = lax.ppermute(last, axis, up)
        after = lax.ppermute(leading, axis, down)
        value = jnp.concatenate([before, value, after], axis=dim)
    return value


def greet_all(n, n_lon, me):
    barrier = pltpu.get_barrier_semaphore()

    def signal(step, carry):
        d = lax.rem(me + step, n)
        pl.semaphore_signal(
            barrier, inc=1, device_id=(d // n_lon, lax.rem(d, n_lon)), device_id_type=MESH
        )
        return carry

    lax.fori_loop(1, n, signal, 0)
    pl.semaphore_wait(barrier, n - 1)


def push(src, dst, send_sem, recv_sem, d, n_lon):
    return pltpu.make_async_remote_copy(
        src_ref=src,
        dst_ref=dst,
        send_sem=send_sem,
        recv_sem=recv_sem,
        device_id=(d // n_lon, lax.rem(d, n_lon)),
        device_id_type=MESH,
    )


def reduce_kernel(
    n_lat, n_lon, x_ref, out_ref, half, pair, parts, total, gath, s0, r0, s1, r1, s2, r2, s3, r3
):
    f32 = jnp.float32
    lat = lax.axis_index("lat")
    lon = lax.axis_index("lon")
    side = lax.rem(lon, 2)
    mate = lon + 1 - 2 * side
    wide = n_lon // 2
    n = n_lat * wide
    me = lat * wide + lon // 2

    def place(g):
        return (g // wide, lax.rem(g, wide) * 2 + side)

    barrier = pltpu.get_barrier_semaphore()
    pl.semaphore_signal(barrier, inc=1, device_id=(lat, mate), device_id_type=MESH)

    def signal(step, carry):
        pl.semaphore_signal(
            barrier, inc=1, device_id=place(lax.rem(me + step, n)), device_id_type=MESH
        )
        return carry

    lax.fori_loop(1, n, signal, 0)
    pl.semaphore_wait(barrier, n)

    def copy(src, dst, send_sem, recv_sem, where):
        return pltpu.make_async_remote_copy(
            src_ref=src,
            dst_ref=dst,
            send_sem=send_sem,
            recv_sem=recv_sem,
            device_id=where,
            device_id_type=MESH,
        )

    first = copy(x_ref.at[1 - side], half, s0, r0, (lat, mate))
    first.start()
    first.wait()

    def scatter(step, carry):
        g = lax.rem(me + step, n)
        pair[g] = (x_ref[side, g].astype(f32) + half[g].astype(f32)).astype(pair.dtype)
        copy(pair.at[g], parts.at[me], s1.at[g], r1.at[me], place(g)).start()
        return carry

    lax.fori_loop(1, n, scatter, 0)

    def add(step, acc):
        g = lax.rem(me + n - step, n)
        copy(pair.at[g], parts.at[g], s1.at[g], r1.at[g], place(g)).wait_recv()
        return acc + parts[g].astype(f32)

    own = x_ref[side, me].astype(f32) + half[me].astype(f32)
    total[...] = lax.fori_loop(1, n, add, own).astype(total.dtype)

    def spread(step, carry):
        g = lax.rem(me + step, n)
        copy(total, gath.at[side, me], s2.at[g], r2.at[me], place(g)).start()
        return carry

    lax.fori_loop(1, n, spread, 0)
    gath[side, me] = total[...]

    def collect(step, carry):
        g = lax.rem(me + n - step, n)
        copy(total, gath.at[side, g], s2.at[g], r2.at[g], place(g)).wait_recv()
        return carry

    lax.fori_loop(1, n, collect, 0)
    last = copy(gath.at[side], gath.at[side], s3, r3, (lat, mate))
    last.start()
    out_ref[side] = gath[side].astype(f32)
    last.wait_send()
    copy(gath.at[1 - side], gath.at[1 - side], s3, r3, (lat, mate)).wait_recv()
    out_ref[1 - side] = gath[1 - side].astype(f32)

    def drain(step, carry):
        g = lax.rem(me + step, n)
        copy(pair.at[g], parts.at[me], s1.at[g], r1.at[me], place(g)).wait_send()
        copy(total, gath.at[side, me], s2.at[g], r2.at[me], place(g)).wait_send()
        return carry

    lax.fori_loop(1, n, drain, 0)


def reduce_all(values, n_lat, n_lon):
    size = values.size
    n = n_lat * n_lon // 2
    rows = -(-size // (128 * 2 * n * 16)) * 16
    flat = jnp.pad(values.reshape(-1), (0, rows * 256 * n - size)).reshape(2, n, rows, 128)
    vmem = pl.BlockSpec(memory_space=pltpu.VMEM)
    dma = pltpu.SemaphoreType.DMA
    slots = pltpu.VMEM((n, rows, 128), jnp.bfloat16)
    out = pl.pallas_call(
        functools.partial(reduce_kernel, n_lat, n_lon),
        out_shape=jax.ShapeDtypeStruct((2, n, rows, 128), jnp.float32),
        in_specs=[vmem],
        out_specs=vmem,
        scratch_shapes=[
            slots,
            slots,
            slots,
            pltpu.VMEM((rows, 128), jnp.bfloat16),
            pltpu.VMEM((2, n, rows, 128), jnp.bfloat16),
            dma,
            dma,
        ]
        + [dma((n,))] * 4
        + [dma, dma],
        compiler_params=pltpu.CompilerParams(
            collective_id=0, has_side_effects=True, vmem_limit_bytes=32 * 2**20
        ),
    )(flat.astype(jnp.bfloat16))
    return out.reshape(-1)[:size].reshape(values.shape)


def spectral_kernel(
    n_lat,
    n_lon,
    own_rows,
    field_ref,
    rim_ref,
    cols_ref,
    leg_ref,
    q_ref,
    ext_ref,
    tab_ref,
    slab,
    table,
    spec,
    gram,
    same,
    msg,
    recv,
    grid,
    back,
    pack,
    legs,
    zeros,
    own_sem,
    s_lon,
    r_lon,
    s_out,
    r_out,
    s_back,
    r_back,
    s_q,
    r_q,
    s_halo,
    r_halo,
):
    f32 = jnp.float32
    bf16 = jnp.bfloat16
    lat = lax.axis_index("lat")
    lon = lax.axis_index("lon")
    n = n_lat * n_lon
    me = lat * n_lon + lon
    rows = msg.shape[1]
    part = rows // own_rows
    band = slab.shape[1]
    lon_cols = band // own_rows
    nlon = lon_cols * n_lon
    greet_all(n, n_lon, me)

    odd = lax.rem(lat, 2)
    sign = 1 - 2 * odd
    hand_to = lat + 2 * sign
    has_other = jnp.logical_and(hand_to >= 0, hand_to < n_lat)
    from_other = lat - 2 * sign
    gets_other = jnp.logical_and(from_other >= 0, from_other < n_lat)
    cut = rim_ref.shape[0] // (16 * PIECES) * 16

    def piece_of(c):
        last = rim_ref.shape[0] - (PIECES - 1) * cut
        return pl.ds(c * cut, cut if c < PIECES - 1 else last)

    def to_mate(c):
        at = piece_of(c)
        return push(
            rim_ref.at[at],
            ext_ref.at[2 * odd, at],
            s_halo.at[c],
            r_halo.at[c],
            (lat + sign) * n_lon + lon,
            n_lon,
        )

    def got_mate(c):
        at = piece_of(c)
        dst = ext_ref.at[2 - 2 * odd, at]
        return push(dst, dst, s_halo.at[c], r_halo.at[c], me, n_lon)

    def hand_on(c):
        at = piece_of(c)
        return push(
            ext_ref.at[2 - 2 * odd, at],
            ext_ref.at[2 * odd, at],
            s_halo.at[PIECES + c],
            r_halo.at[PIECES + c],
            hand_to * n_lon + lon,
            n_lon,
        )

    def relay_halo(c):
        got_mate(c).wait_recv()

        @pl.when(has_other)
        def _():
            hand_on(c).start()

        if c < PIECES - 1:
            to_mate(c + 1).start()

    def to_lon(t):
        src = field_ref.at[pl.ds(pl.multiple_of(t * band, 16), band)]
        return push(src, slab.at[lon], s_lon.at[t], r_lon.at[lon], lat * n_lon + t, n_lon)

    for step in range(n_lon - 1, 0, -1):
        to_lon(lax.rem(lon + step, n_lon)).start()

    to_mate(0).start()
    own_block = pltpu.make_async_copy(rim_ref, ext_ref.at[1], own_sem.at[1])
    own_block.start()
    blank = pltpu.make_async_copy(zeros, ext_ref.at[2 * odd], own_sem.at[2])

    @pl.when(jnp.logical_not(gets_other))
    def _():
        zeros[...] = jnp.zeros_like(zeros)
        blank.start()

    slab[lon] = field_ref[pl.ds(pl.multiple_of(lon * band, 16), band)]

    chunk = 64

    def wave(phase):
        turn = phase - jnp.round(phase * (1.0 / nlon)) * float(nlon)
        x = (0.25 - jnp.abs(turn) * (1.0 / nlon)) * 6.283185307179586
        y = x * x
        p = -2.505210838544172e-8
        for c in SINE:
            p = p * y + c
        return (p * x).astype(bf16)

    def tables(i, carry):
        at = pl.ds(pl.multiple_of(i * chunk, chunk), chunk)
        order = cols_ref[at, 0:1]
        shift = cols_ref[at, 1:2]
        j = lax.broadcasted_iota(jnp.int32, (chunk, lon_cols), 1).astype(f32)
        for s in range(n_lon):
            table[s, at] = wave((j + float(s * lon_cols)) * order + shift)
        tab_ref[1, at] = wave((j + (lon * lon_cols).astype(f32)) * order + (shift + nlon / 4.0))
        return carry

    chunks = table.shape[1] // chunk
    lax.fori_loop(0, chunks // 2, tables, 0)
    relay_halo(0)
    lax.fori_loop(chunks // 2, chunks, tables, 0)
    tab_ref[0] = table[lon]
    relay_halo(1)

    for step in range(n_lon):
        s = lax.rem(lon + step, n_lon)
        if step:
            push(slab.at[s], slab.at[s], s_lon.at[s], r_lon.at[s], me, n_lon).wait_recv()
        wide = slab[s].astype(f32)
        for a in range(own_rows):
            piece = wide[a * lon_cols : (a + 1) * lon_cols].astype(bf16)
            term = jnp.dot(table[s], piece, preferred_element_type=f32)
            if step:
                term = term + spec[a]
            if step == n_lon - 1:
                term = term * cols_ref[:, 2 + a : 3 + a]
            spec[a] = term

    def message(d):
        at = pl.ds(pl.multiple_of(d * part, 8), part)
        return jnp.concatenate([spec[a, at] for a in range(own_rows)], axis=0).astype(bf16)

    def to_owner(d):
        return push(msg.at[d], recv.at[me], s_out.at[d], r_out.at[me], d, n_lon)

    def send_out(step, carry):
        d = lax.rem(me + step, n)
        msg[d] = message(d)
        to_owner(d).start()
        return carry

    lax.fori_loop(1, n, send_out, 0)
    recv[me] = message(me)

    total = gram.shape[0]
    block = same.shape[0]
    kind = lax.rem(lax.broadcasted_iota(jnp.int32, (block, total), 0), part)
    other = lax.rem(lax.broadcasted_iota(jnp.int32, (block, total), 1), part)
    same[...] = jnp.where(kind == other, 1.0, 0.0)

    nlat = n_lat * own_rows * n_lon
    own = part // 2

    def spread_rows(i, carry):
        at = pl.ds(pl.multiple_of(i * block, 16), block)
        row = i * block + lax.broadcasted_iota(jnp.int32, (block, 1), 0)
        wanted = lax.rem(row, own) * nlat + lax.div(row, part)
        column = lax.broadcasted_iota(jnp.int32, (block, leg_ref.shape[0]), 1)
        pick = jnp.where(column == wanted, 1.0, 0.0).astype(bf16)
        legs[at] = jnp.dot(pick, leg_ref[...], preferred_element_type=f32).astype(bf16)
        return carry

    lax.fori_loop(0, total // block, spread_rows, 0)

    def grams(i, carry):
        at = pl.ds(pl.multiple_of(i * block, 16), block)
        product = lax.dot_general(
            legs[at], legs[...], (((1,), (1,)), ((), ())), preferred_element_type=f32
        )
        gram[at] = (product * same[...]).astype(bf16)
        return carry

    lax.fori_loop(0, total // block, grams, 0)

    def await_out(step, carry):
        d = lax.rem(me + n - step, n)
        push(msg.at[d], recv.at[d], s_out.at[d], r_out.at[d], d, n_lon).wait_recv()
        return carry

    lax.fori_loop(1, n, await_out, 0)
    relay_halo(2)

    per = block // rows
    blocks = total // block

    def to_rows(d):
        return push(grid.at[d], back.at[me], s_back.at[d], r_back.at[me], d, n_lon)

    def send_back(i, carry):
        b = lax.rem(me // per + 1 + i, blocks)
        at = pl.ds(pl.multiple_of(b * block, 16), block)
        value = jnp.dot(
            gram[at], recv[...].reshape(total, recv.shape[2]), preferred_element_type=f32
        ).astype(bf16)
        for e in range(per):
            d = b * per + e
            grid[d] = value[e * rows : (e + 1) * rows]

            @pl.when(d != me)
            def _():
                to_rows(d).start()

        return carry

    lax.fori_loop(0, blocks, send_back, 0)
    back[me] = grid[me]

    span = n_lon * part

    def group(i):
        g = lax.rem(lat + 2 * n_lat - 1 - i, n_lat)
        return g, pl.ds(pl.multiple_of(g * span, 16), span)

    def to_slab(t, g, at):
        return push(
            pack.at[:, at],
            q_ref.at[lon, :, at],
            s_q.at[t, g],
            r_q.at[lon, g],
            lat * n_lon + t,
            n_lon,
        )

    def got(t, g, at, slot):
        dst = q_ref.at[t, :, at]
        return push(dst, dst, s_q.at[t, g], r_q.at[slot, g], me, n_lon)

    half = n_lon // 2
    cross = lax.rem(lon + half, n_lon)
    side = lax.rem(lon, half)
    mate = lon - side + (half - 1 - side)
    far = lax.rem(mate + half, n_lon)
    paired = n_lon == 4
    targets = (cross, mate) if paired else [lax.rem(lon + e, n_lon) for e in range(1, n_lon)]

    def relay(g, at):
        dst = q_ref.at[cross, :, at]
        return push(dst, dst, s_q.at[far, g], r_q.at[n_lon, g], lat * n_lon + mate, n_lon)

    def gather(i, carry):
        g, at = group(i)
        for e in range(n_lon):
            d = g * n_lon + e

            @pl.when(d != me)
            def _():
                push(grid.at[d], back.at[d], s_back.at[d], r_back.at[d], d, n_lon).wait_recv()

        wide = back[pl.ds(g * n_lon, n_lon)].astype(f32)
        for a in range(own_rows):
            rows_a = wide[:, a * part : (a + 1) * part]
            pack[a, at] = rows_a.reshape(span, wide.shape[2]).astype(bf16)
        for t in targets:
            to_slab(t, g, at).start()
        return carry

    lax.fori_loop(0, n_lat, gather, 0)
    relay_halo(3)
    keep = pltpu.make_async_copy(pack, q_ref.at[lon], own_sem.at[0])
    keep.start()

    def hand_over(i, carry):
        g, at = group(i)
        got(cross, g, at, cross).wait_recv()
        relay(g, at).start()
        return carry

    def finish(i, carry):
        g, at = group(i)
        for t in targets:
            to_slab(t, g, at).wait_send()
        if paired:
            got(mate, g, at, mate).wait_recv()
            got(far, g, at, n_lon).wait_recv()
            relay(g, at).wait_send()
        else:
            for t in targets:
                got(t, g, at, t).wait_recv()
        return carry

    if paired:
        lax.fori_loop(0, n_lat, hand_over, 0)
    lax.fori_loop(0, n_lat, finish, 0)
    keep.wait()

    for step in range(1, n_lon):
        to_lon(lax.rem(lon + step, n_lon)).wait_send()

    def drain(step, carry):
        d = lax.rem(me + step, n)
        to_owner(d).wait_send()
        to_rows(d).wait_send()
        return carry

    lax.fori_loop(1, n, drain, 0)

    own_block.wait()

    @pl.when(jnp.logical_not(gets_other))
    def _():
        blank.wait()

    for c in range(PIECES):
        to_mate(c).wait_send()

        @pl.when(has_other)
        def _():
            hand_on(c).wait_send()

        @pl.when(gets_other)
        def _():
            dst = ext_ref.at[2 * odd, piece_of(c)]
            push(dst, dst, s_halo.at[PIECES + c], r_halo.at[PIECES + c], me, n_lon).wait_recv()


def spectral(field, rimmed, cols, leg, n_lat, n_lon, own_rows):
    lat_rows, lon_cols, channels = field.shape
    n = n_lat * n_lon
    total = 2 * leg.shape[0]
    rows = total // n
    bf16 = jnp.bfloat16
    f32 = jnp.float32
    band = own_rows * lon_cols
    q_rows = cols.shape[0]
    block = total // 8
    vmem = pl.BlockSpec(memory_space=pltpu.VMEM)
    anywhere = pl.BlockSpec(memory_space=pl.ANY)
    dma = pltpu.SemaphoreType.DMA
    flat_rim = rimmed.reshape(-1, channels)
    return pl.pallas_call(
        functools.partial(spectral_kernel, n_lat, n_lon, own_rows),
        out_shape=(
            jax.ShapeDtypeStruct((n_lon, own_rows, q_rows, channels), bf16),
            jax.ShapeDtypeStruct((3,) + flat_rim.shape, bf16),
            jax.ShapeDtypeStruct((2, q_rows, lon_cols), bf16),
        ),
        in_specs=[vmem, anywhere, vmem, vmem],
        out_specs=(anywhere, anywhere, vmem),
        scratch_shapes=[
            pltpu.VMEM((n_lon, band, channels), bf16),
            pltpu.VMEM((n_lon, q_rows, lon_cols), bf16),
            pltpu.VMEM((own_rows, q_rows, channels), f32),
            pltpu.VMEM((total, total), bf16),
            pltpu.VMEM((block, total), f32),
        ]
        + [pltpu.VMEM((n, rows, channels), bf16)] * 4
        + [pltpu.VMEM((own_rows, q_rows, channels), bf16), pltpu.VMEM((total, leg.shape[1]), bf16)]
        + [pltpu.VMEM(flat_rim.shape, bf16), dma((3,))]
        + [dma((n_lon,))] * 2
        + [dma((n,))] * 4
        + [dma((n_lon, n_lat)), dma((n_lon + 1, n_lat))]
        + [dma((2 * PIECES,))] * 2,
        compiler_params=pltpu.CompilerParams(
            collective_id=1, has_side_effects=True, vmem_limit_bytes=52 * 2**20
        ),
    )(field.reshape(-1, channels), flat_rim, cols, leg)


def outer_sum(left, right):
    return lax.dot_general(
        left, right, (((0,), (0,)), ((), ())), preferred_element_type=jnp.float32
    )


def local(
    field,
    cotangent,
    legendre,
    quad_weight,
    order_slots,
    support_blocks,
    filter_values,
    spectral_weight,
    disco_weight,
):
    f32 = jnp.float32
    bf16 = jnp.bfloat16
    lat_rows, lon_cols, channels = field.shape
    n_lon = lax.axis_size("lon")
    n_dev = n_lon * lax.axis_size("lat")
    nlon = lon_cols * n_lon
    slots_dev, nlat, degrees = legendre.shape
    own_rows = lat_rows // n_lon
    lat_pos = lax.axis_index("lat")
    lon_pos = lax.axis_index("lon")
    own = -(-slots_dev // n_lon)
    pad = own * n_lon - slots_dev

    orders = order_slots.reshape(-1, slots_dev)
    orders = jnp.pad(orders, ((0, 0), (0, pad))).reshape(n_dev, own)
    flat_orders = orders.reshape(-1)
    own_leg = jnp.pad(legendre, ((0, pad), (0, 0), (0, 0)))
    own_leg = lax.dynamic_slice_in_dim(own_leg, lon_pos * own, own)
    own_orders = lax.dynamic_slice_in_dim(orders, lat_pos * n_lon + lon_pos, 1)[0]
    mask = jnp.arange(degrees, dtype=jnp.int32)[None, :] >= own_orders[:, None]
    masked = jnp.where(mask[:, None, :], own_leg, jnp.zeros((), bf16))
    own_quad = lax.dynamic_slice_in_dim(quad_weight, lon_pos * own_rows, own_rows)
    rimmed = padded(field, (("lon", 1),), 1, True)
    rimmed = jnp.pad(rimmed, ((0, 0), (0, -rimmed.shape[1] % 16), (0, 0)))
    if own % 4 == 0 and n_dev * own % 64 == 0 and own_rows * lon_cols % 16 == 0:
        shape = (n_dev, 2, own)
        factor = jnp.where(orders == 0, 1.0, 2.0)[:, None, :] / nlon
        cols = [
            jnp.broadcast_to(orders[:, None, :].astype(f32), shape),
            jnp.broadcast_to(jnp.array([0.0, nlon / 4], f32)[None, :, None], shape),
        ]
        cols += [jnp.broadcast_to(factor * own_quad[a], shape) for a in range(own_rows)]
        cols = jnp.stack([c.reshape(-1) for c in cols], axis=1)
        leg = masked.reshape(-1, degrees)
        grid, halo, direct = spectral(field, rimmed, cols, leg, lax.axis_size("lat"), n_lon, own_rows)
        grid = grid.reshape(lat_rows, -1, channels)
        waves = [
            jnp.einsum("qj,aqc->ajc", piece, grid, preferred_element_type=f32).astype(bf16)
            for piece in (direct[0], direct[1])
        ]
        extended = halo.reshape(3 * lat_rows, -1, channels)
    else:
        column = jnp.arange(nlon, dtype=jnp.int32)
        phase = column[:, None] * flat_orders[None, :] % nlon
        angle = phase.astype(f32) * (2.0 * jnp.pi / nlon)
        cosine = jnp.cos(angle).astype(bf16).reshape(nlon, n_dev, own)
        sine = (-jnp.sin(angle)).astype(bf16).reshape(nlon, n_dev, own)
        table = jnp.stack([cosine, sine], axis=2)
        factor = jnp.where(flat_orders == 0, 1.0, 2.0).astype(bf16).reshape(n_dev, own)
        gram = jnp.einsum("kal,kbl->kab", own_leg, masked, preferred_element_type=f32).astype(bf16)

        parts = field.reshape(n_lon, own_rows, lon_cols, channels)
        slabs = lax.all_to_all(parts, "lon", split_axis=0, concat_axis=0, tiled=True)
        slabs = slabs.transpose(1, 0, 2, 3).reshape(own_rows, nlon, channels)
        spectrum = jnp.einsum(
            "ajc,jq->aqc", slabs, table.reshape(nlon, -1), preferred_element_type=f32
        )
        spectrum = (spectrum * (own_quad * (1.0 / nlon))[:, None, None]).astype(bf16)
        spectrum = spectrum.reshape(own_rows, n_dev, 2 * own, channels).transpose(1, 0, 2, 3)
        gathered = lax.all_to_all(spectrum, BOTH, split_axis=0, concat_axis=0, tiled=True)
        gathered = gathered.reshape(nlat, 2, own, channels)
        grid = jnp.einsum("kab,brkc->arkc", gram, gathered, preferred_element_type=f32).astype(bf16)
        grid = grid.reshape(n_dev, own_rows, 2 * own, channels)
        grid = lax.all_to_all(grid, BOTH, split_axis=0, concat_axis=0, tiled=True)
        grid = grid.transpose(1, 0, 2, 3).reshape(own_rows, n_dev * 2 * own, channels)
        grid = lax.all_gather(grid, "lon", axis=0, tiled=True)

        here = lax.dynamic_slice_in_dim(table, lon_pos * lon_cols, lon_cols)
        here = here * factor[None, :, None, :]
        turned = jnp.stack([here[:, :, 1], -here[:, :, 0]], axis=2)
        direct = here.reshape(lon_cols, -1)
        turned = turned.reshape(lon_cols, -1)
        waves = [
            jnp.einsum("jq,aqc->ajc", piece, grid, preferred_element_type=f32).astype(bf16)
            for piece in (direct, turned)
        ]
        extended = padded(rimmed, (("lat", 0),), lat_rows, False)

    picks = support_blocks[0] - lat_pos + 1
    onehot = (picks[:, None] == jnp.arange(3, dtype=jnp.int32)[None, :]).astype(f32)
    operator = (
        jnp.einsum("tasb,sq->taqb", filter_values.astype(f32), onehot)
        .reshape(3, lat_rows, 3 * lat_rows)
        .astype(bf16)
    )
    responses = []
    for tap in range(3):
        window = extended[:, tap : tap + lon_cols]
        responses.append(
            jnp.einsum("ab,boc->aoc", operator[tap], window, preferred_element_type=f32).astype(
                bf16
            )
        )
    sources = [v.reshape(-1, channels) for v in waves + responses]
    weights = [spectral_weight[0], spectral_weight[1]] + [disco_weight[t] for t in range(3)]
    pre_act = sum(
        jnp.dot(s, w, preferred_element_type=f32) for s, w in zip(sources, weights)
    ).reshape(lat_rows, lon_cols, channels)
    activated, pullback = jax.vjp(jax.nn.gelu, pre_act)
    output = (field.astype(f32) + activated).astype(bf16)
    (grad_pre,) = pullback(cotangent.astype(f32))
    flat_grad = grad_pre.astype(bf16).reshape(-1, channels)
    grads = jnp.concatenate([outer_sum(s, flat_grad) for s in sources], axis=0)
    total = reduce_all(grads.reshape(5, channels, channels), lax.axis_size("lat"), n_lon)
    return (output, total[:2], total[2:])


def solution(mesh):
    placed = (
        P("lat", "lon", None),
        P("lat", "lon", None),
        P("lat", None, None),
        P("lat"),
        P(),
        P("lat", None),
        P(None, "lat", None, None),
        P(),
        P(),
    )
    return jax.shard_map(
        local,
        mesh=mesh,
        in_specs=placed,
        out_specs=(P("lat", "lon", None), P(), P()),
        check_vma=False,
    )
```

```python
import functools

import jax
import jax.numpy as jnp
from jax import lax
from jax.experimental import pallas as pl
from jax.experimental.pallas import tpu as pltpu
from jax.sharding import PartitionSpec as P

MESH = pl.DeviceIdType.MESH
PIECES = 4
SINE = (2.7557319223985893e-6, -1.984126984126984e-4, 8.333333333333333e-3, -1 / 6, 1.0)

BOTH = ("lat", "lon")


def padded(value, sides, width, wrap):
    for axis, dim in sides:
        size, length = (lax.axis_size(axis), value.shape[dim])
        up = [(i, (i + 1) % size) for i in range(size if wrap else size - 1)]
        down = [(j, i) for i, j in up]
        last = lax.slice_in_dim(value, length - width, length, axis=dim)
        leading = lax.slice_in_dim(value, 0, width, axis=dim)
        before = lax.ppermute(last, axis, up)
        after = lax.ppermute(leading, axis, down)
        value = jnp.concatenate([before, value, after], axis=dim)
    return value


def greet_all(n, n_lon, me):
    barrier = pltpu.get_barrier_semaphore()

    def signal(step, carry):
        d = lax.rem(me + step, n)
        pl.semaphore_signal(
            barrier, inc=1, device_id=(d // n_lon, lax.rem(d, n_lon)), device_id_type=MESH
        )
        return carry

    lax.fori_loop(1, n, signal, 0)
    pl.semaphore_wait(barrier, n - 1)


def push(src, dst, send_sem, recv_sem, d, n_lon):
    return pltpu.make_async_remote_copy(
        src_ref=src,
        dst_ref=dst,
        send_sem=send_sem,
        recv_sem=recv_sem,
        device_id=(d // n_lon, lax.rem(d, n_lon)),
        device_id_type=MESH,
    )


def reduce_kernel(
    n_lat, n_lon, x_ref, out_ref, half, pair, parts, total, gath, s0, r0, s1, r1, s2, r2, s3, r3
):
    f32 = jnp.float32
    lat = lax.axis_index("lat")
    lon = lax.axis_index("lon")
    side = lax.rem(lon, 2)
    mate = lon + 1 - 2 * side
    wide = n_lon // 2
    n = n_lat * wide
    me = lat * wide + lon // 2

    def place(g):
        return (g // wide, lax.rem(g, wide) * 2 + side)

    barrier = pltpu.get_barrier_semaphore()
    pl.semaphore_signal(barrier, inc=1, device_id=(lat, mate), device_id_type=MESH)

    def signal(step, carry):
        pl.semaphore_signal(
            barrier, inc=1, device_id=place(lax.rem(me + step, n)), device_id_type=MESH
        )
        return carry

    lax.fori_loop(1, n, signal, 0)
    pl.semaphore_wait(barrier, n)

    def copy(src, dst, send_sem, recv_sem, where):
        return pltpu.make_async_remote_copy(
            src_ref=src,
            dst_ref=dst,
            send_sem=send_sem,
            recv_sem=recv_sem,
            device_id=where,
            device_id_type=MESH,
        )

    first = copy(x_ref.at[1 - side], half, s0, r0, (lat, mate))
    first.start()
    first.wait()

    def scatter(step, carry):
        g = lax.rem(me + step, n)
        pair[g] = (x_ref[side, g].astype(f32) + half[g].astype(f32)).astype(pair.dtype)
        copy(pair.at[g], parts.at[me], s1.at[g], r1.at[me], place(g)).start()
        return carry

    lax.fori_loop(1, n, scatter, 0)

    def add(step, acc):
        g = lax.rem(me + n - step, n)
        copy(pair.at[g], parts.at[g], s1.at[g], r1.at[g], place(g)).wait_recv()
        return acc + parts[g].astype(f32)

    own = x_ref[side, me].astype(f32) + half[me].astype(f32)
    total[...] = lax.fori_loop(1, n, add, own).astype(total.dtype)

    def spread(step, carry):
        g = lax.rem(me + step, n)
        copy(total, gath.at[side, me], s2.at[g], r2.at[me], place(g)).start()
        return carry

    lax.fori_loop(1, n, spread, 0)
    gath[side, me] = total[...]

    def collect(step, carry):
        g = lax.rem(me + n - step, n)
        copy(total, gath.at[side, g], s2.at[g], r2.at[g], place(g)).wait_recv()
        return carry

    lax.fori_loop(1, n, collect, 0)
    last = copy(gath.at[side], gath.at[side], s3, r3, (lat, mate))
    last.start()
    out_ref[side] = gath[side].astype(f32)
    last.wait_send()
    copy(gath.at[1 - side], gath.at[1 - side], s3, r3, (lat, mate)).wait_recv()
    out_ref[1 - side] = gath[1 - side].astype(f32)

    def drain(step, carry):
        g = lax.rem(me + step, n)
        copy(pair.at[g], parts.at[me], s1.at[g], r1.at[me], place(g)).wait_send()
        copy(total, gath.at[side, me], s2.at[g], r2.at[me], place(g)).wait_send()
        return carry

    lax.fori_loop(1, n, drain, 0)


def reduce_all(values, n_lat, n_lon):
    size = values.size
    n = n_lat * n_lon // 2
    rows = -(-size // (128 * 2 * n * 16)) * 16
    flat = jnp.pad(values.reshape(-1), (0, rows * 256 * n - size)).reshape(2, n, rows, 128)
    vmem = pl.BlockSpec(memory_space=pltpu.VMEM)
    dma = pltpu.SemaphoreType.DMA
    slots = pltpu.VMEM((n, rows, 128), jnp.bfloat16)
    out = pl.pallas_call(
        functools.partial(reduce_kernel, n_lat, n_lon),
        out_shape=jax.ShapeDtypeStruct((2, n, rows, 128), jnp.float32),
        in_specs=[vmem],
        out_specs=vmem,
        scratch_shapes=[
            slots,
            slots,
            slots,
            pltpu.VMEM((rows, 128), jnp.bfloat16),
            pltpu.VMEM((2, n, rows, 128), jnp.bfloat16),
            dma,
            dma,
        ]
        + [dma((n,))] * 4
        + [dma, dma],
        compiler_params=pltpu.CompilerParams(
            collective_id=0, has_side_effects=True, vmem_limit_bytes=32 * 2**20
        ),
    )(flat.astype(jnp.bfloat16))
    return out.reshape(-1)[:size].reshape(values.shape)


def spectral_kernel(
    n_lat,
    n_lon,
    own_rows,
    field_ref,
    rim_ref,
    cols_ref,
    leg_ref,
    q_ref,
    ext_ref,
    tab_ref,
    slab,
    table,
    spec,
    gram,
    same,
    msg,
    recv,
    grid,
    back,
    pack,
    legs,
    zeros,
    own_sem,
    s_lon,
    r_lon,
    s_out,
    r_out,
    s_back,
    r_back,
    s_q,
    r_q,
    s_halo,
    r_halo,
):
    f32 = jnp.float32
    bf16 = jnp.bfloat16
    lat = lax.axis_index("lat")
    lon = lax.axis_index("lon")
    n = n_lat * n_lon
    me = lat * n_lon + lon
    rows = msg.shape[1]
    part = rows // own_rows
    band = slab.shape[1]
    lon_cols = band // own_rows
    nlon = lon_cols * n_lon
    greet_all(n, n_lon, me)

    odd = lax.rem(lat, 2)
    sign = 1 - 2 * odd
    hand_to = lat + 2 * sign
    has_other = jnp.logical_and(hand_to >= 0, hand_to < n_lat)
    from_other = lat - 2 * sign
    gets_other = jnp.logical_and(from_other >= 0, from_other < n_lat)
    cut = rim_ref.shape[0] // (16 * PIECES) * 16

    def piece_of(c):
        last = rim_ref.shape[0] - (PIECES - 1) * cut
        return pl.ds(c * cut, cut if c < PIECES - 1 else last)

    def to_mate(c):
        at = piece_of(c)
        return push(
            rim_ref.at[at],
            ext_ref.at[2 * odd, at],
            s_halo.at[c],
            r_halo.at[c],
            (lat + sign) * n_lon + lon,
            n_lon,
        )

    def got_mate(c):
        at = piece_of(c)
        dst = ext_ref.at[2 - 2 * odd, at]
        return push(dst, dst, s_halo.at[c], r_halo.at[c], me, n_lon)

    def hand_on(c):
        at = piece_of(c)
        return push(
            ext_ref.at[2 - 2 * odd, at],
            ext_ref.at[2 * odd, at],
            s_halo.at[PIECES + c],
            r_halo.at[PIECES + c],
            hand_to * n_lon + lon,
            n_lon,
        )

    def relay_halo(c):
        got_mate(c).wait_recv()

        @pl.when(has_other)
        def _():
            hand_on(c).start()

        if c < PIECES - 1:
            to_mate(c + 1).start()

    def to_lon(t):
        src = field_ref.at[pl.ds(pl.multiple_of(t * band, 16), band)]
        return push(src, slab.at[lon], s_lon.at[t], r_lon.at[lon], lat * n_lon + t, n_lon)

    for step in range(n_lon - 1, 0, -1):
        to_lon(lax.rem(lon + step, n_lon)).start()

    to_mate(0).start()
    own_block = pltpu.make_async_copy(rim_ref, ext_ref.at[1], own_sem.at[1])
    own_block.start()
    blank = pltpu.make_async_copy(zeros, ext_ref.at[2 * odd], own_sem.at[2])

    @pl.when(jnp.logical_not(gets_other))
    def _():
        zeros[...] = jnp.zeros_like(zeros)
        blank.start()

    slab[lon] = field_ref[pl.ds(pl.multiple_of(lon * band, 16), band)]

    chunk = 64

    def wave(phase):
        turn = phase - jnp.round(phase * (1.0 / nlon)) * float(nlon)
        x = (0.25 - jnp.abs(turn) * (1.0 / nlon)) * 6.283185307179586
        y = x * x
        p = -2.505210838544172e-8
        for c in SINE:
            p = p * y + c
        return (p * x).astype(bf16)

    def tables(i, carry):
        at = pl.ds(pl.multiple_of(i * chunk, chunk), chunk)
        order = cols_ref[at, 0:1]
        shift = cols_ref[at, 1:2]
        j = lax.broadcasted_iota(jnp.int32, (chunk, lon_cols), 1).astype(f32)
        for s in range(n_lon):
            table[s, at] = wave((j + float(s * lon_cols)) * order + shift)
        tab_ref[1, at] = wave((j + (lon * lon_cols).astype(f32)) * order + (shift + nlon / 4.0))
        return carry

    chunks = table.shape[1] // chunk
    lax.fori_loop(0, chunks // 2, tables, 0)
    relay_halo(0)
    lax.fori_loop(chunks // 2, chunks, tables, 0)
    tab_ref[0] = table[lon]

    for step in range(n_lon):
        s = lax.rem(lon + step, n_lon)
        if step:
            push(slab.at[s], slab.at[s], s_lon.at[s], r_lon.at[s], me, n_lon).wait_recv()
        wide = slab[s].astype(f32)
        for a in range(own_rows):
            piece = wide[a * lon_cols : (a + 1) * lon_cols].astype(bf16)
            term = jnp.dot(table[s], piece, preferred_element_type=f32)
            if step:
                term = term + spec[a]
            if step == n_lon - 1:
                term = term * cols_ref[:, 2 + a : 3 + a]
            spec[a] = term

    def message(d):
        at = pl.ds(pl.multiple_of(d * part, 8), part)
        return jnp.concatenate([spec[a, at] for a in range(own_rows)], axis=0).astype(bf16)

    def to_owner(d):
        return push(msg.at[d], recv.at[me], s_out.at[d], r_out.at[me], d, n_lon)

    def send_out(step, carry):
        d = lax.rem(me + step, n)
        msg[d] = message(d)
        to_owner(d).start()
        return carry

    lax.fori_loop(1, n, send_out, 0)
    recv[me] = message(me)
    relay_halo(1)

    total = gram.shape[0]
    block = same.shape[0]
    kind = lax.rem(lax.broadcasted_iota(jnp.int32, (block, total), 0), part)
    other = lax.rem(lax.broadcasted_iota(jnp.int32, (block, total), 1), part)
    same[...] = jnp.where(kind == other, 1.0, 0.0)

    nlat = n_lat * own_rows * n_lon
    own = part // 2

    def spread_rows(i, carry):
        at = pl.ds(pl.multiple_of(i * block, 16), block)
        row = i * block + lax.broadcasted_iota(jnp.int32, (block, 1), 0)
        wanted = lax.rem(row, own) * nlat + lax.div(row, part)
        column = lax.broadcasted_iota(jnp.int32, (block, leg_ref.shape[0]), 1)
        pick = jnp.where(column == wanted, 1.0, 0.0).astype(bf16)
        legs[at] = jnp.dot(pick, leg_ref[...], preferred_element_type=f32).astype(bf16)
        return carry

    lax.fori_loop(0, total // block, spread_rows, 0)

    def grams(i, carry):
        at = pl.ds(pl.multiple_of(i * block, 16), block)
        product = lax.dot_general(
            legs[at], legs[...], (((1,), (1,)), ((), ())), preferred_element_type=f32
        )
        gram[at] = (product * same[...]).astype(bf16)
        return carry

    lax.fori_loop(0, total // block, grams, 0)

    def await_out(step, carry):
        d = lax.rem(me + n - step, n)
        push(msg.at[d], recv.at[d], s_out.at[d], r_out.at[d], d, n_lon).wait_recv()
        return carry

    lax.fori_loop(1, n, await_out, 0)
    relay_halo(2)

    per = block // rows
    blocks = total // block

    def to_rows(d):
        return push(grid.at[d], back.at[me], s_back.at[d], r_back.at[me], d, n_lon)

    def send_back(i, carry):
        b = lax.rem(me // per + 1 + i, blocks)
        at = pl.ds(pl.multiple_of(b * block, 16), block)
        value = jnp.dot(
            gram[at], recv[...].reshape(total, recv.shape[2]), preferred_element_type=f32
        ).astype(bf16)
        for e in range(per):
            d = b * per + e
            grid[d] = value[e * rows : (e + 1) * rows]

            @pl.when(d != me)
            def _():
                to_rows(d).start()

        return carry

    lax.fori_loop(0, blocks, send_back, 0)
    back[me] = grid[me]

    span = n_lon * part

    def group(i):
        g = lax.rem(lat + 2 * n_lat - 1 - i, n_lat)
        return g, pl.ds(pl.multiple_of(g * span, 16), span)

    def to_slab(t, g, at):
        return push(
            pack.at[:, at],
            q_ref.at[lon, :, at],
            s_q.at[t, g],
            r_q.at[lon, g],
            lat * n_lon + t,
            n_lon,
        )

    def got(t, g, at, slot):
        dst = q_ref.at[t, :, at]
        return push(dst, dst, s_q.at[t, g], r_q.at[slot, g], me, n_lon)

    half = n_lon // 2
    cross = lax.rem(lon + half, n_lon)
    side = lax.rem(lon, half)
    mate = lon - side + (half - 1 - side)
    far = lax.rem(mate + half, n_lon)
    paired = n_lon == 4
    targets = (cross, mate) if paired else [lax.rem(lon + e, n_lon) for e in range(1, n_lon)]

    def relay(g, at):
        dst = q_ref.at[cross, :, at]
        return push(dst, dst, s_q.at[far, g], r_q.at[n_lon, g], lat * n_lon + mate, n_lon)

    def gather(i, carry):
        g, at = group(i)
        for e in range(n_lon):
            d = g * n_lon + e

            @pl.when(d != me)
            def _():
                push(grid.at[d], back.at[d], s_back.at[d], r_back.at[d], d, n_lon).wait_recv()

        wide = back[pl.ds(g * n_lon, n_lon)].astype(f32)
        for a in range(own_rows):
            rows_a = wide[:, a * part : (a + 1) * part]
            pack[a, at] = rows_a.reshape(span, wide.shape[2]).astype(bf16)
        for t in targets:
            to_slab(t, g, at).start()
        return carry

    lax.fori_loop(0, n_lat, gather, 0)
    relay_halo(3)
    keep = pltpu.make_async_copy(pack, q_ref.at[lon], own_sem.at[0])
    keep.start()

    def hand_over(i, carry):
        g, at = group(i)
        got(cross, g, at, cross).wait_recv()
        relay(g, at).start()
        return carry

    def finish(i, carry):
        g, at = group(i)
        for t in targets:
            to_slab(t, g, at).wait_send()
        if paired:
            got(mate, g, at, mate).wait_recv()
            got(far, g, at, n_lon).wait_recv()
            relay(g, at).wait_send()
        else:
            for t in targets:
                got(t, g, at, t).wait_recv()
        return carry

    if paired:
        lax.fori_loop(0, n_lat, hand_over, 0)
    lax.fori_loop(0, n_lat, finish, 0)
    keep.wait()

    for step in range(1, n_lon):
        to_lon(lax.rem(lon + step, n_lon)).wait_send()

    def drain(step, carry):
        d = lax.rem(me + step, n)
        to_owner(d).wait_send()
        to_rows(d).wait_send()
        return carry

    lax.fori_loop(1, n, drain, 0)

    own_block.wait()

    @pl.when(jnp.logical_not(gets_other))
    def _():
        blank.wait()

    for c in range(PIECES):
        to_mate(c).wait_send()

        @pl.when(has_other)
        def _():
            hand_on(c).wait_send()

        @pl.when(gets_other)
        def _():
            dst = ext_ref.at[2 * odd, piece_of(c)]
            push(dst, dst, s_halo.at[PIECES + c], r_halo.at[PIECES + c], me, n_lon).wait_recv()


def spectral(field, rimmed, cols, leg, n_lat, n_lon, own_rows):
    lat_rows, lon_cols, channels = field.shape
    n = n_lat * n_lon
    total = 2 * leg.shape[0]
    rows = total // n
    bf16 = jnp.bfloat16
    f32 = jnp.float32
    band = own_rows * lon_cols
    q_rows = cols.shape[0]
    block = total // 8
    vmem = pl.BlockSpec(memory_space=pltpu.VMEM)
    anywhere = pl.BlockSpec(memory_space=pl.ANY)
    dma = pltpu.SemaphoreType.DMA
    flat_rim = rimmed.reshape(-1, channels)
    return pl.pallas_call(
        functools.partial(spectral_kernel, n_lat, n_lon, own_rows),
        out_shape=(
            jax.ShapeDtypeStruct((n_lon, own_rows, q_rows, channels), bf16),
            jax.ShapeDtypeStruct((3,) + flat_rim.shape, bf16),
            jax.ShapeDtypeStruct((2, q_rows, lon_cols), bf16),
        ),
        in_specs=[vmem, anywhere, vmem, vmem],
        out_specs=(anywhere, anywhere, vmem),
        scratch_shapes=[
            pltpu.VMEM((n_lon, band, channels), bf16),
            pltpu.VMEM((n_lon, q_rows, lon_cols), bf16),
            pltpu.VMEM((own_rows, q_rows, channels), f32),
            pltpu.VMEM((total, total), bf16),
            pltpu.VMEM((block, total), f32),
        ]
        + [pltpu.VMEM((n, rows, channels), bf16)] * 4
        + [pltpu.VMEM((own_rows, q_rows, channels), bf16), pltpu.VMEM((total, leg.shape[1]), bf16)]
        + [pltpu.VMEM(flat_rim.shape, bf16), dma((3,))]
        + [dma((n_lon,))] * 2
        + [dma((n,))] * 4
        + [dma((n_lon, n_lat)), dma((n_lon + 1, n_lat))]
        + [dma((2 * PIECES,))] * 2,
        compiler_params=pltpu.CompilerParams(
            collective_id=1, has_side_effects=True, vmem_limit_bytes=52 * 2**20
        ),
    )(field.reshape(-1, channels), flat_rim, cols, leg)


def outer_sum(left, right):
    return lax.dot_general(
        left, right, (((0,), (0,)), ((), ())), preferred_element_type=jnp.float32
    )


def local(
    field,
    cotangent,
    legendre,
    quad_weight,
    order_slots,
    support_blocks,
    filter_values,
    spectral_weight,
    disco_weight,
):
    f32 = jnp.float32
    bf16 = jnp.bfloat16
    lat_rows, lon_cols, channels = field.shape
    n_lon = lax.axis_size("lon")
    n_dev = n_lon * lax.axis_size("lat")
    nlon = lon_cols * n_lon
    slots_dev, nlat, degrees = legendre.shape
    own_rows = lat_rows // n_lon
    lat_pos = lax.axis_index("lat")
    lon_pos = lax.axis_index("lon")
    own = -(-slots_dev // n_lon)
    pad = own * n_lon - slots_dev

    orders = order_slots.reshape(-1, slots_dev)
    orders = jnp.pad(orders, ((0, 0), (0, pad))).reshape(n_dev, own)
    flat_orders = orders.reshape(-1)
    own_leg = jnp.pad(legendre, ((0, pad), (0, 0), (0, 0)))
    own_leg = lax.dynamic_slice_in_dim(own_leg, lon_pos * own, own)
    own_orders = lax.dynamic_slice_in_dim(orders, lat_pos * n_lon + lon_pos, 1)[0]
    mask = jnp.arange(degrees, dtype=jnp.int32)[None, :] >= own_orders[:, None]
    masked = jnp.where(mask[:, None, :], own_leg, jnp.zeros((), bf16))
    own_quad = lax.dynamic_slice_in_dim(quad_weight, lon_pos * own_rows, own_rows)
    rimmed = padded(field, (("lon", 1),), 1, True)
    rimmed = jnp.pad(rimmed, ((0, 0), (0, -rimmed.shape[1] % 16), (0, 0)))
    if own % 4 == 0 and n_dev * own % 64 == 0 and own_rows * lon_cols % 16 == 0:
        shape = (n_dev, 2, own)
        factor = jnp.where(orders == 0, 1.0, 2.0)[:, None, :] / nlon
        cols = [
            jnp.broadcast_to(orders[:, None, :].astype(f32), shape),
            jnp.broadcast_to(jnp.array([0.0, nlon / 4], f32)[None, :, None], shape),
        ]
        cols += [jnp.broadcast_to(factor * own_quad[a], shape) for a in range(own_rows)]
        cols = jnp.stack([c.reshape(-1) for c in cols], axis=1)
        leg = masked.reshape(-1, degrees)
        grid, halo, direct = spectral(field, rimmed, cols, leg, lax.axis_size("lat"), n_lon, own_rows)
        grid = grid.reshape(lat_rows, -1, channels)
        waves = [
            jnp.einsum("qj,aqc->ajc", piece, grid, preferred_element_type=f32).astype(bf16)
            for piece in (direct[0], direct[1])
        ]
        extended = halo.reshape(3 * lat_rows, -1, channels)
    else:
        column = jnp.arange(nlon, dtype=jnp.int32)
        phase = column[:, None] * flat_orders[None, :] % nlon
        angle = phase.astype(f32) * (2.0 * jnp.pi / nlon)
        cosine = jnp.cos(angle).astype(bf16).reshape(nlon, n_dev, own)
        sine = (-jnp.sin(angle)).astype(bf16).reshape(nlon, n_dev, own)
        table = jnp.stack([cosine, sine], axis=2)
        factor = jnp.where(flat_orders == 0, 1.0, 2.0).astype(bf16).reshape(n_dev, own)
        gram = jnp.einsum("kal,kbl->kab", own_leg, masked, preferred_element_type=f32).astype(bf16)

        parts = field.reshape(n_lon, own_rows, lon_cols, channels)
        slabs = lax.all_to_all(parts, "lon", split_axis=0, concat_axis=0, tiled=True)
        slabs = slabs.transpose(1, 0, 2, 3).reshape(own_rows, nlon, channels)
        spectrum = jnp.einsum(
            "ajc,jq->aqc", slabs, table.reshape(nlon, -1), preferred_element_type=f32
        )
        spectrum = (spectrum * (own_quad * (1.0 / nlon))[:, None, None]).astype(bf16)
        spectrum = spectrum.reshape(own_rows, n_dev, 2 * own, channels).transpose(1, 0, 2, 3)
        gathered = lax.all_to_all(spectrum, BOTH, split_axis=0, concat_axis=0, tiled=True)
        gathered = gathered.reshape(nlat, 2, own, channels)
        grid = jnp.einsum("kab,brkc->arkc", gram, gathered, preferred_element_type=f32).astype(bf16)
        grid = grid.reshape(n_dev, own_rows, 2 * own, channels)
        grid = lax.all_to_all(grid, BOTH, split_axis=0, concat_axis=0, tiled=True)
        grid = grid.transpose(1, 0, 2, 3).reshape(own_rows, n_dev * 2 * own, channels)
        grid = lax.all_gather(grid, "lon", axis=0, tiled=True)

        here = lax.dynamic_slice_in_dim(table, lon_pos * lon_cols, lon_cols)
        here = here * factor[None, :, None, :]
        turned = jnp.stack([here[:, :, 1], -here[:, :, 0]], axis=2)
        direct = here.reshape(lon_cols, -1)
        turned = turned.reshape(lon_cols, -1)
        waves = [
            jnp.einsum("jq,aqc->ajc", piece, grid, preferred_element_type=f32).astype(bf16)
            for piece in (direct, turned)
        ]
        extended = padded(rimmed, (("lat", 0),), lat_rows, False)

    picks = support_blocks[0] - lat_pos + 1
    onehot = (picks[:, None] == jnp.arange(3, dtype=jnp.int32)[None, :]).astype(f32)
    operator = (
        jnp.einsum("tasb,sq->taqb", filter_values.astype(f32), onehot)
        .reshape(3, lat_rows, 3 * lat_rows)
        .astype(bf16)
    )
    responses = []
    for tap in range(3):
        window = extended[:, tap : tap + lon_cols]
        responses.append(
            jnp.einsum("ab,boc->aoc", operator[tap], window, preferred_element_type=f32).astype(
                bf16
            )
        )
    sources = [v.reshape(-1, channels) for v in waves + responses]
    weights = [spectral_weight[0], spectral_weight[1]] + [disco_weight[t] for t in range(3)]
    pre_act = sum(
        jnp.dot(s, w, preferred_element_type=f32) for s, w in zip(sources, weights)
    ).reshape(lat_rows, lon_cols, channels)
    activated, pullback = jax.vjp(jax.nn.gelu, pre_act)
    output = (field.astype(f32) + activated).astype(bf16)
    (grad_pre,) = pullback(cotangent.astype(f32))
    flat_grad = grad_pre.astype(bf16).reshape(-1, channels)
    grads = jnp.concatenate([outer_sum(s, flat_grad) for s in sources], axis=0)
    total = reduce_all(grads.reshape(5, channels, channels), lax.axis_size("lat"), n_lon)
    return (output, total[:2], total[2:])


def solution(mesh):
    placed = (
        P("lat", "lon", None),
        P("lat", "lon", None),
        P("lat", None, None),
        P("lat"),
        P(),
        P("lat", None),
        P(None, "lat", None, None),
        P(),
        P(),
    )
    return jax.shard_map(
        local,
        mesh=mesh,
        in_specs=placed,
        out_specs=(P("lat", "lon", None), P(), P()),
        check_vma=False,
    )
```
